32 devices in a mesh: dp: 8 (over z, x), tensor: 4 (over y, core).
Axes of the slice: x: 2, y: 2, z: 4, core: 2. Of those that a mesh axis runs over, the one named last changes fastest.
Arguments:
- patch_rows: bfloat16 [256, 32, 768], P('tensor', 'dp'), may hold values from -6 to 6
- cotangent: bfloat16 [256, 32, 768], P('tensor', 'dp'), may hold values from -6 to 6
- mask_flags: int32 [256, 32], P('tensor', 'dp'), may hold values from 0 to 1, as said below
- pad_flags: int32 [256, 32], P(None, 'dp'), may hold values from 0 to 1, as said below
- buckets: int32 [256, 256], replicated, may hold values from 0 to 731, as said below
- mask_emb: bfloat16 [768], replicated, may hold values from -6 to 6
- ln1_gain: bfloat16 [2, 768], replicated, may hold values from 0.5 to 1.5
- ln1_bias: bfloat16 [2, 768], replicated, may hold values from -1.75 to 1.75
- w_qkv: bfloat16 [2, 3, 768, 768], P(None, None, None, 'tensor'), may hold values from -0.21875 to 0.21875
- qv_bias: bfloat16 [2, 2, 768], P(None, None, 'tensor'), may hold values from -3 to 3
- rel_table: bfloat16 [2, 12, 732], P(None, 'tensor'), may hold values from -6 to 6
- w_out: bfloat16 [2, 768, 768], P(None, 'tensor'), may hold values from -0.625 to 0.625
- out_bias: bfloat16 [2, 768], replicated, may hold values from -1.75 to 1.75
- ln2_gain: bfloat16 [2, 768], replicated, may hold values from 0.5 to 1.5
- ln2_bias: bfloat16 [2, 768], replicated, may hold values from -1.75 to 1.75
- w_up: bfloat16 [2, 768, 3072], P(None, None, 'tensor'), may hold values from -0.21875 to 0.21875
- up_bias: bfloat16 [2, 3072], P(None, 'tensor'), may hold values from -1.75 to 1.75
- w_down: bfloat16 [2, 3072, 768], P(None, 'tensor'), may hold values from -0.109375 to 0.109375
- down_bias: bfloat16 [2, 768], replicated, may hold values from -1.75 to 1.75
Outputs:
- layer_out: bfloat16 [256, 32, 768], P('tensor', 'dp')
- d_x: float32 [256, 32, 768], P('tensor', 'dp')
- d_mask_emb: float32 [768], replicated
- d_ln1_gain: float32 [2, 768], replicated
- d_ln1_bias: float32 [2, 768], replicated
- d_w_qkv: float32 [2, 3, 768, 768], P(None, None, None, 'tensor')
- d_qv_bias: float32 [2, 2, 768], P(None, None, 'tensor')
- d_rel_table: float32 [2, 12, 732], P(None, 'tensor')
- d_w_out: float32 [2, 768, 768], P(None, 'tensor')
- d_out_bias: float32 [2, 768], replicated
- d_ln2_gain: float32 [2, 768], replicated
- d_ln2_bias: float32 [2, 768], replicated
- d_w_up: float32 [2, 768, 3072], P(None, None, 'tensor')
- d_up_bias: float32 [2, 3072], P(None, 'tensor')
- d_w_down: float32 [2, 3072, 768], P(None, 'tensor')
- d_down_bias: float32 [2, 768], replicated
The draws below stay inside these ranges and needn't reach their ends.
Inputs may be any that keep to these rules, and one draw needn't show every extreme that they name: `mask_flags`: each page has its own masking rate, drawn from 20 to 60 percent. `pad_flags`: in each page the rows from its patch count on are 1, the patch count between 160 and 197. `buckets`: the bucket depends only on the two rows' places in the 14 x 14 patch grid, or on class or padding rows.
All inputs are finite; a program needn't handle non-finite values.
Results may differ from the reference program's by a relative error of at most 0.025.
Values may be sent and summed in bfloat16 or wider, within the bound.
No kernel may reach another device: no remote copies, remote signals or barrier semaphores. Data moves between devices by JAX's collectives and lax.ppermute only.
A program may use at most 192 MiB of HBM per device.

```python
import jax
import jax.numpy as jnp
from jax import lax

D = 768
HEADS = 12
HEAD_DIM = 64
FF = 3072
SEQ = 256
PATCHES = 197
GRID = 14
LEN_LO = 160
BUCKETS = 732
LAYERS = 2
PAGES_DEV = 4
PAGES = 32
N_DP = 8


def draw_mask_flags(key, part):
    key = jax.random.fold_in(key, 11)
    rate_key, roll_key = jax.random.split(key)
    rates = jax.random.randint(rate_key, (1, PAGES), 20, 61)
    rolls = jax.random.randint(roll_key, (SEQ, PAGES), 0, 100)
    return (rolls < rates).astype(jnp.int32)


def draw_pad_flags(key, part):
    key = jax.random.fold_in(key, 23)
    lengths = jax.random.randint(key, (1, PAGES), LEN_LO, PATCHES + 1)
    positions = lax.broadcasted_iota(jnp.int32, (SEQ, PAGES), 0)
    return (positions >= lengths).astype(jnp.int32)


def draw_buckets(key, part):
    key = jax.random.fold_in(key, 37)
    span_size = 2 * GRID - 1
    positions = jnp.arange(SEQ, dtype=jnp.int32)
    is_patch = (positions >= 1) & (positions < PATCHES)
    cell_index = jnp.clip(positions - 1, 0, GRID * GRID - 1)
    grid_row = cell_index // GRID
    grid_col = cell_index % GRID
    relative = (grid_row[:, None] - grid_row[None, :] + GRID - 1) * span_size + (grid_col[:, None] - grid_col[None, :] + GRID - 1)
    both_patch = is_patch[:, None] & is_patch[None, :]
    query_patch = jnp.broadcast_to(is_patch[:, None], (SEQ, SEQ))
    key_patch = jnp.broadcast_to(is_patch[None, :], (SEQ, SEQ))
    base_index = jnp.where(both_patch, relative, jnp.where(query_patch, BUCKETS - 3, jnp.where(key_patch, BUCKETS - 2, BUCKETS - 1)))
    ordering = jax.random.permutation(key, BUCKETS).astype(jnp.int32)
    return ordering[base_index].astype(jnp.int32)


def level_of(stream_key, extent, cuts, low, largest):
    gain, own = 1.0, jax.random.fold_in(stream_key, 6)
    for position, blocks in cuts:
        steps = jnp.exp(jax.random.uniform(jax.random.fold_in(own, position), (blocks,), jnp.float32, low / len(cuts), largest / len(cuts)))
        gain = gain * jnp.repeat(steps, extent[position] // blocks).reshape([-1 if axis == position else 1 for axis in range(len(extent))])
    return gain


def gaussian(key, dims, width, reach, cuts=(), kind=jnp.bfloat16):
    entries = width * jax.random.normal(key, dims, jnp.float32)
    if cuts:
        entries = entries * level_of(key, dims, cuts, -0.22, 0.18)
    return jnp.clip(entries, -reach, reach).astype(kind)


def setup_inputs(seed: int = 0) -> dict:
    splits = jax.random.split(jax.random.key(seed), 20)
    return {
        "patch_rows": gaussian(splits[0], (SEQ, PAGES, D), 1.0, 6.0, ((0, 4), (1, 8))),
        "cotangent": gaussian(splits[1], (SEQ, PAGES, D), 1.0, 6.0, ((0, 4), (1, 8))),
        "mask_flags": draw_mask_flags(jax.random.fold_in(splits[19], 71), 0),
        "pad_flags": draw_pad_flags(jax.random.fold_in(splits[19], 71), 0),
        "buckets": draw_buckets(jax.random.fold_in(splits[19], 71), 0),
        "mask_emb": gaussian(splits[5], (D,), 1.0, 6.0),
        "ln1_gain": jnp.clip(1.0 + 0.1 * jax.random.normal(splits[6], (LAYERS, D), jnp.float32), 0.5, 1.5).astype(jnp.bfloat16),
        "ln1_bias": gaussian(splits[7], (LAYERS, D), 0.3, 1.75),
        "w_qkv": gaussian(splits[8], (LAYERS, 3, D, D), D ** -0.5, 0.21875, ((3, 4),)),
        "qv_bias": gaussian(splits[9], (LAYERS, 2, D), 0.5, 3.0, ((2, 4),)),
        "rel_table": gaussian(splits[10], (LAYERS, HEADS, BUCKETS), 1.0, 6.0, ((1, 4),)),
        "w_out": gaussian(splits[11], (LAYERS, D, D), (D // 8) ** -0.5, 0.625, ((1, 4),)),
        "out_bias": gaussian(splits[12], (LAYERS, D), 0.3, 1.75),
        "ln2_gain": jnp.clip(1.0 + 0.1 * jax.random.normal(splits[13], (LAYERS, D), jnp.float32), 0.5, 1.5).astype(jnp.bfloat16),
        "ln2_bias": gaussian(splits[14], (LAYERS, D), 0.3, 1.75),
        "w_up": gaussian(splits[15], (LAYERS, D, FF), D ** -0.5, 0.21875, ((2, 4),)),
        "up_bias": gaussian(splits[16], (LAYERS, FF), 0.3, 1.75, ((1, 4),)),
        "w_down": gaussian(splits[17], (LAYERS, FF, D), FF ** -0.5, 0.109375, ((1, 4),)),
        "down_bias": gaussian(splits[18], (LAYERS, D), 0.3, 1.75),
    }


EPSILON = 1e-06
HIGHEST_PRECISION = lax.Precision.HIGHEST

@jax.custom_vjp
def low(v):
    return lax.optimization_barrier(v.astype(jnp.bfloat16)).astype(jnp.float32)

@jax.custom_vjp
def low_back(v):
    return v

def low_keep(v):
    return (low(v), None)

def low_pass(kept, grad):
    return (grad,)

def back_keep(v):
    return (v, None)

def back_low(kept, grad):
    return (low(grad),)
low.defvjp(low_keep, low_pass)
low_back.defvjp(back_keep, back_low)

def norm_rows(values, norm_gain, norm_shift):
    center = values - lax.optimization_barrier(jnp.mean(values, axis=-1, keepdims=True))
    spread = lax.optimization_barrier(jnp.mean(center * center, axis=-1, keepdims=True))
    return center * lax.rsqrt(spread + EPSILON) * norm_gain + norm_shift

def product(einsum_form, left_side, right_side):
    return jnp.einsum(einsum_form, left_side, right_side, precision=HIGHEST_PRECISION)

def one_layer(hidden, params, layer_index, key_bias, buckets):
    seq_rows, page_count, model_width = hidden.shape
    query_scale = HEAD_DIM ** (-0.5)
    head_shape = (seq_rows, page_count, HEADS, HEAD_DIM)
    normed = low(norm_rows(hidden, params['ln1_gain'][layer_index], params['ln1_bias'][layer_index]))
    w_qkv = params['w_qkv'][layer_index]
    qv_bias = params['qv_bias'][layer_index]
    queries = low_back(low((product('spd,de->spe', normed, w_qkv[0]) + qv_bias[0]) * query_scale))
    key_rows = low_back(low(product('spd,de->spe', normed, w_qkv[1])))
    value_rows = low_back(low(product('spd,de->spe', normed, w_qkv[2]) + qv_bias[1]))
    queries = queries.reshape(head_shape)
    key_rows = key_rows.reshape(head_shape)
    value_rows = value_rows.reshape(head_shape)
    rel_bias = params['rel_table'][layer_index][:, buckets]
    scores = low_back(product('qphe,kphe->phqk', queries, key_rows) + rel_bias[None] + key_bias)
    softmax_weights = low(jax.nn.softmax(scores, axis=-1))
    attended = product('phqk,kphe->qphe', softmax_weights, value_rows).reshape(seq_rows, page_count, model_width)
    attended = low_back(low(attended))
    after_mixer = hidden + low_back(product('spe,ed->spd', attended, params['w_out'][layer_index])) + params['out_bias'][layer_index]
    normed_two = low(norm_rows(after_mixer, params['ln2_gain'][layer_index], params['ln2_bias'][layer_index]))
    pre_act = low_back(product('spd,df->spf', normed_two, params['w_up'][layer_index]) + params['up_bias'][layer_index])
    activated = low(jax.nn.gelu(pre_act, approximate=True))
    return after_mixer + low_back(product('spf,fd->spd', activated, params['w_down'][layer_index])) + params['down_bias'][layer_index]

def forward(params, inputs, mask_vector, masked, key_bias, buckets):
    hidden = jnp.where(masked, mask_vector, inputs)
    for layer_index in range(LAYERS):
        hidden = one_layer(hidden, params, layer_index, key_bias, buckets)
    return hidden

def reference(patch_rows, cotangent, mask_flags, pad_flags, buckets, mask_emb, ln1_gain, ln1_bias, w_qkv, qv_bias, rel_table, w_out, out_bias, ln2_gain, ln2_bias, w_up, up_bias, w_down, down_bias):
    params = {'ln1_gain': ln1_gain.astype(jnp.float32), 'ln1_bias': ln1_bias.astype(jnp.float32), 'w_qkv': w_qkv.astype(jnp.float32), 'qv_bias': qv_bias.astype(jnp.float32), 'rel_table': rel_table.astype(jnp.float32), 'w_out': w_out.astype(jnp.float32), 'out_bias': out_bias.astype(jnp.float32), 'ln2_gain': ln2_gain.astype(jnp.float32), 'ln2_bias': ln2_bias.astype(jnp.float32), 'w_up': w_up.astype(jnp.float32), 'up_bias': up_bias.astype(jnp.float32), 'w_down': w_down.astype(jnp.float32), 'down_bias': down_bias.astype(jnp.float32)}
    mask_vector = mask_emb.astype(jnp.float32)

    def split_pages(values):
        return jnp.moveaxis(values.reshape((SEQ, N_DP, PAGES_DEV) + values.shape[2:]), 1, 0)

    def join_pages(values):
        return jnp.moveaxis(values, 0, 1).reshape((SEQ, PAGES) + values.shape[3:])
    zero_grads = jax.tree.map(jnp.zeros_like, params)

    def group_step(carry, members):
        grads, mask_grad = carry
        inputs, cot_rows, flag_rows, pad_rows = members
        masked = (flag_rows == 1)[..., None]
        key_bias = jnp.where(pad_rows == 1, -1000000000.0, 0.0).astype(jnp.float32).T[:, None, None, :]

        def run_forward(param_tree, layer_inputs, embedding):
            return forward(param_tree, layer_inputs, embedding, masked, key_bias, buckets)
        outputs, pull_back = jax.vjp(run_forward, params, inputs, mask_vector)
        grad_params, grad_inputs, grad_mask = pull_back(cot_rows)
        grads = jax.tree.map(jnp.add, grads, grad_params)
        return ((grads, mask_grad + grad_mask), (outputs, grad_inputs))
    members = (split_pages(patch_rows.astype(jnp.float32)), split_pages(cotangent.astype(jnp.float32)), split_pages(mask_flags), split_pages(pad_flags))
    (grads, mask_grad), (outputs, grad_inputs) = lax.scan(group_step, (zero_grads, jnp.zeros((D,), jnp.float32)), members)
    return (join_pages(outputs).astype(jnp.bfloat16), join_pages(grad_inputs), mask_grad, grads['ln1_gain'], grads['ln1_bias'], grads['w_qkv'], grads['qv_bias'], grads['rel_table'], grads['w_out'], grads['out_bias'], grads['ln2_gain'], grads['ln2_bias'], grads['w_up'], grads['up_bias'], grads['w_down'], grads['down_bias'])
```

```python
import functools

import jax
import jax.numpy as jnp
from jax import lax
from jax.experimental import pallas as pl
from jax.experimental.pallas import tpu as pltpu
from jax.sharding import PartitionSpec as P

HEAD_DIM = 64
BUCKETS = 732
LAYERS = 2
EPSILON = 1e-06
GROUPS = 1

BF = jnp.bfloat16
F32 = jnp.float32
CORE = [(i, i ^ 1) for i in range(4)]
CHIP = [(i, i ^ 2) for i in range(4)]
VMEM = pl.BlockSpec(memory_space=pltpu.VMEM)


def swap_core(values):
    return lax.ppermute(values, "tensor", CORE)


def swap_chip(values):
    return lax.ppermute(values, "tensor", CHIP)


def spread(own):
    far = swap_chip(own)
    near = swap_core(own)
    return [own, near, far, swap_core(far)]


def collect(partial):
    pair_far = partial[2] + swap_core(partial[3])
    arriving = swap_chip(pair_far)
    pair_own = partial[0].astype(F32) + swap_core(partial[1]).astype(F32)
    return pair_own + arriving.astype(F32)


def own_order(values, axis, member):
    low, high = member & 1, member >> 1

    def taken(source, order):
        return jnp.concatenate([lax.slice_in_dim(source, i, i + 1, axis=axis) for i in order], axis)

    values = jnp.where(low == 1, taken(values, (1, 0, 3, 2)), values)
    return jnp.where(high == 1, taken(values, (2, 3, 0, 1)), values)


def bias_kernel(table_ref, index_ref, out_ref):
    tables, chunks, lanes = table_ref.shape

    def rows_step(step, carry):
        rows = pl.ds(pl.multiple_of(step * 16, 16), 16)
        for half in range(2):
            columns = slice(half * 128, half * 128 + 128)
            index = index_ref[rows, columns]
            lane, chunk = index & 127, index >> 7
            here = [chunk == c for c in range(chunks)]
            for member in range(tables):
                total = jnp.zeros((16, 128), F32)
                for c in range(chunks):
                    line = jnp.broadcast_to(table_ref[member, c : c + 1, :], (16, 128))
                    total = jnp.where(here[c], jnp.take_along_axis(line, lane, axis=1), total)
                out_ref[member, rows, columns] = total.astype(out_ref.dtype)
        return carry

    lax.fori_loop(0, index_ref.shape[0] // 16, rows_step, 0)


def bias_of_buckets(tables, buckets):
    count, entries = tables.shape
    chunks = (entries + 127) // 128
    padded = jnp.pad(tables.astype(F32), ((0, 0), (0, chunks * 128 - entries)))
    return pl.pallas_call(
        bias_kernel,
        out_shape=jax.ShapeDtypeStruct((count,) + buckets.shape, BF),
        in_specs=[VMEM, VMEM],
        out_specs=VMEM,
        name="bias_of_buckets",
        cost_estimate=pl.CostEstimate(flops=10_000_000, bytes_accessed=1_500_000, transcendentals=0),
    )(padded.reshape(count, chunks, 128), buckets)


def bucket_kernel(values_ref, index_ref, out_ref):
    heads, size, width = values_ref.shape
    chunk = 8

    def step(i, total):
        start = pl.multiple_of(i * chunk, chunk)
        index = index_ref[pl.ds(start, chunk), :]
        left, right = [], []
        for r in range(chunk):
            row = index[r : r + 1, :]
            at_high = lax.broadcasted_iota(jnp.int32, (24, width), 0) == (row >> 5)
            at_low = lax.broadcasted_iota(jnp.int32, (32, width), 0) == (row & 31)
            right.append(jnp.where(at_low, 1.0, 0.0).astype(BF))
            left.append(
                jnp.concatenate(
                    [
                        jnp.where(at_high, values_ref[h, pl.ds(start + r, 1), :], 0.0).astype(BF)
                        for h in range(heads)
                    ],
                    0,
                )
            )
        return total + lax.dot_general(
            jnp.concatenate(left, 1),
            jnp.concatenate(right, 1),
            (((1,), (1,)), ((), ())),
            preferred_element_type=F32,
        )

    out_ref[...] = lax.fori_loop(0, size // chunk, step, jnp.zeros((heads * 24, 32), F32))


def sum_by_bucket(values, buckets):
    heads = values.shape[0]
    out = pl.pallas_call(
        bucket_kernel,
        out_shape=jax.ShapeDtypeStruct((heads * 24, 32), F32),
        in_specs=[VMEM, VMEM],
        out_specs=VMEM,
        name="sum_by_bucket",
        cost_estimate=pl.CostEstimate(flops=2_000_000_000, bytes_accessed=1_000_000, transcendentals=0),
    )(values, buckets)
    return out.reshape(heads, 768)


def norm_stats(values):
    mean = jnp.mean(values, axis=-1, keepdims=True)
    center = values - mean
    inverse = lax.rsqrt(jnp.mean(center * center, axis=-1, keepdims=True) + EPSILON)
    return center * inverse, inverse


def norm_rows(values, gain, shift):
    normal, unused = norm_stats(values)
    return (normal * gain + shift).astype(BF)


def norm_back(grad, values, gain):
    normal, inverse = norm_stats(values)
    scaled = grad * gain
    inner = scaled - jnp.mean(scaled, -1, keepdims=True) - normal * jnp.mean(scaled * normal, -1, keepdims=True)
    return inner * inverse, jnp.sum(grad * normal, axis=(0, 1)), jnp.sum(grad, axis=(0, 1))


def dot(form, left, right):
    return jnp.einsum(form, left, right, preferred_element_type=F32)


def joined(blocks):
    return jnp.concatenate(blocks, axis=1)


def parted(values):
    return jnp.split(values, 4, axis=1)


def gelu_tanh(values):
    return jax.nn.gelu(values, approximate=True)


def scores_of(queries, keys, rel_bias, key_bias):
    return dot("pqhe,pkhe->phqk", queries, keys) + rel_bias[None].astype(F32) + key_bias


def attention_in(own, w, key_bias):
    rows_all = joined(spread(own))
    pages, length, unused = rows_all.shape
    projected = dot("psd,tde->pste", rows_all, w["w_qkv"])
    shape = (pages, length, -1, HEAD_DIM)
    q = ((projected[:, :, 0] + w["qv_bias"][0]) * HEAD_DIM**-0.5).astype(BF).reshape(shape)
    k = projected[:, :, 1].astype(BF).reshape(shape)
    v = (projected[:, :, 2] + w["qv_bias"][1]).astype(BF).reshape(shape)
    scores = scores_of(q, k, w["rel_bias"], key_bias)
    row_max = jnp.max(scores, axis=-1, keepdims=True)
    log_total = row_max + jnp.log(jnp.sum(jnp.exp(scores - row_max), axis=-1, keepdims=True))
    weights = jnp.exp(scores - log_total).astype(BF)
    o = dot("phqk,pkhe->pqhe", weights, v).reshape(pages, length, -1).astype(BF)
    mixed = dot("pse,ed->psd", o, w["w_out"]).astype(BF)
    return mixed, (rows_all, q, k, v, log_total, o)


def attention_back(grad_all, kept, w, key_bias):
    rows_all, q, k, v, log_total, o = kept
    go = dot("psd,ed->pse", grad_all, w["w_out"]).astype(BF).reshape(q.shape)
    p = jnp.exp(scores_of(q, k, w["rel_bias"], key_bias) - log_total)
    gv = dot("phqk,pqhe->pkhe", p.astype(BF), go).astype(BF)
    gp = dot("pqhe,pkhe->phqk", go, v)
    gs = (p * (gp - jnp.sum(p * gp, axis=-1, keepdims=True))).astype(BF)
    totals = jnp.sum(gs.astype(F32), axis=0)
    gq = dot("phqk,pkhe->pqhe", gs, k).astype(BF) * HEAD_DIM**-0.5
    gk = dot("phqk,pqhe->pkhe", gs, q).astype(BF)
    flat = o.shape
    stacked = jnp.concatenate([gq.reshape(flat), gk.reshape(flat), gv.reshape(flat)], axis=-1)
    w_joined = jnp.concatenate([w["w_qkv"][i] for i in range(3)], axis=-1)
    ga = dot("pse,de->psd", stacked, w_joined).astype(BF)
    return ga, stacked, totals


def butterfly_reduce(values, bits, place):
    order = []
    for bit in bits:
        half = values.shape[0] // 2
        mine = (place >> bit) & 1
        first, second = values[:half], values[half:]
        keep = jnp.where(mine == 1, second, first)
        send = jnp.where(mine == 1, first, second)
        got = lax.ppermute(send, "dp", [(i, i ^ (1 << bit)) for i in range(1 << len(bits))])
        values = keep + got
    return values


def butterfly_gather(values, bits, place):
    for bit in reversed(bits):
        mine = (place >> bit) & 1
        got = lax.ppermute(values, "dp", [(i, i ^ (1 << bit)) for i in range(1 << len(bits))])
        values = jnp.concatenate(
            [jnp.where(mine == 1, got, values), jnp.where(mine == 1, values, got)], axis=0
        )
    return values


def sum_pages(values, bits, place):
    return butterfly_gather(butterfly_reduce(values, bits, place), bits, place)


def sum_small(values, axis, bits):
    for bit in bits:
        values = values + lax.ppermute(values, axis, [(i, i ^ (1 << bit)) for i in range(1 << len(bits))])
    return values


def shards(
    n_dp,
    patch_rows,
    cotangent,
    mask_flags,
    pad_flags,
    buckets,
    mask_emb,
    ln1_gain,
    ln1_bias,
    w_qkv,
    qv_bias,
    rel_table,
    w_out,
    out_bias,
    ln2_gain,
    ln2_bias,
    w_up,
    up_bias,
    w_down,
    down_bias,
):
    member = lax.axis_index("tensor")
    place = lax.axis_index("dp")
    bits = list(range(n_dp.bit_length() - 1))
    positions, pages, width = patch_rows.shape
    per_group = pages // GROUPS
    heads = rel_table.shape[1]

    length = buckets.shape[0]
    ordered = own_order(buckets.reshape(4, positions, 4, positions), 0, member)
    ordered = own_order(ordered, 2, member).reshape(length, length)
    pads = own_order(pad_flags.reshape(4, positions, pages), 0, member).reshape(length, pages)
    key_bias = jnp.where(pads == 1, -1000000000.0, 0.0).astype(F32).T[:, None, None, :]
    rel_bias = bias_of_buckets(rel_table.reshape(LAYERS * heads, BUCKETS), ordered)
    rel_bias = rel_bias.reshape(LAYERS, heads, length, length)

    def by_page(values):
        return jnp.swapaxes(values, 0, 1)

    masked = by_page(mask_flags == 1)[..., None]
    rows = by_page(patch_rows).astype(F32)
    hidden_all = jnp.where(masked, mask_emb.astype(F32), rows)
    cotangent = by_page(cotangent)

    def weights_of(layer):
        return {
            "ln1_gain": ln1_gain[layer].astype(F32),
            "ln1_bias": ln1_bias[layer].astype(F32),
            "w_qkv": w_qkv[layer],
            "qv_bias": qv_bias[layer].astype(F32),
            "rel_bias": rel_bias[layer],
            "w_out": w_out[layer],
            "out_bias": out_bias[layer].astype(F32),
            "ln2_gain": ln2_gain[layer].astype(F32),
            "ln2_bias": ln2_bias[layer].astype(F32),
            "w_up": w_up[layer],
            "up_bias": up_bias[layer].astype(F32),
            "w_down": w_down[layer],
            "down_bias": down_bias[layer].astype(F32),
        }

    groups = range(GROUPS)

    def part(values, g):
        return values[g * per_group : (g + 1) * per_group]

    weights = [weights_of(layer) for layer in range(LAYERS)]
    hidden = [part(hidden_all, g) for g in groups]
    pads_of = [part(key_bias, g) for g in groups]
    last_grad = [joined(spread(part(cotangent, g))) for g in groups]
    kept = []
    for layer in range(LAYERS):
        w = weights[layer]
        saved = []
        for g in groups:
            own = norm_rows(hidden[g], w["ln1_gain"], w["ln1_bias"])
            mixed, kept_attention = attention_in(own, w, pads_of[g])
            middle = hidden[g] + collect(parted(mixed)) + w["out_bias"]
            own = norm_rows(middle, w["ln2_gain"], w["ln2_bias"])
            rows_two = joined(spread(own))
            u = dot("psd,df->psf", rows_two, w["w_up"]) + w["up_bias"]
            z = gelu_tanh(u).astype(BF)
            down = dot("psf,fd->psd", z, w["w_down"]).astype(BF)
            saved.append((hidden[g], kept_attention, middle, rows_two, u, z))
            hidden[g] = middle + collect(parted(down)) + w["down_bias"]
        kept.append(saved)
    result = jnp.concatenate([h.astype(BF) for h in hidden], axis=0)

    grads = [part(cotangent, g).astype(F32) for g in groups]
    large = [None] * LAYERS
    slim = [None] * LAYERS
    small = [None] * LAYERS
    for layer in reversed(range(LAYERS)):
        w = weights[layer]
        d_down_bias = sum(jnp.sum(grads[g], axis=(0, 1)) for g in groups)
        stage = []
        d_up_bias = 0.0
        for g in groups:
            before, kept_attention, middle, rows_two, u, z = kept[layer][g]
            gm = last_grad[g] if layer == LAYERS - 1 else joined(spread(grads[g].astype(BF)))
            gz = dot("psd,fd->psf", gm, w["w_down"])
            unused, pull = jax.vjp(gelu_tanh, u)
            gu = pull(gz)[0].astype(BF)
            d_up_bias = d_up_bias + jnp.sum(gu.astype(F32), axis=(0, 1))
            gc = dot("psf,df->psd", gu, w["w_up"]).astype(BF)
            stage.append((gm, gu, collect(parted(gc))))
        d_w_down = sum(dot("psf,psd->fd", kept[layer][g][5], stage[g][0]) for g in groups)
        d_w_up = sum(dot("psd,psf->df", kept[layer][g][3], stage[g][1]) for g in groups)
        d_ln2_gain = d_ln2_bias = d_out_bias = 0.0
        second = []
        for g in groups:
            before, kept_attention, middle, rows_two, u, z = kept[layer][g]
            inner, d_gain, d_shift = norm_back(stage[g][2], middle, w["ln2_gain"])
            g1 = grads[g] + inner
            d_ln2_gain, d_ln2_bias = d_ln2_gain + d_gain, d_ln2_bias + d_shift
            d_out_bias = d_out_bias + jnp.sum(g1, axis=(0, 1))
            gr = joined(spread(g1.astype(BF)))
            ga, stacked, totals = attention_back(gr, kept_attention, w, pads_of[g])
            second.append((g1, gr, stacked, totals, collect(parted(ga))))
        mlp_sum = sum_pages(jnp.concatenate([d_w_down, d_w_up], axis=0).astype(BF), bits, place)
        d_w_out = sum(dot("pse,psd->ed", kept[layer][g][1][5], second[g][1]) for g in groups)
        d_w_qkv = sum(dot("pse,psd->ed", second[g][2], kept[layer][g][1][0]) for g in groups)
        attention_sum = sum_pages(jnp.concatenate([d_w_out, d_w_qkv], axis=0).astype(BF), bits, place)
        d_rel = sum_by_bucket(sum(second[g][3] for g in groups), ordered)[:, :BUCKETS]
        flat_sum = sum(jnp.sum(second[g][2].astype(F32), axis=(0, 1)) for g in groups)
        d_ln1_gain = d_ln1_bias = 0.0
        for g in groups:
            inner, d_gain, d_shift = norm_back(second[g][4], kept[layer][g][0], w["ln1_gain"])
            grads[g] = second[g][0] + inner
            d_ln1_gain, d_ln1_bias = d_ln1_gain + d_gain, d_ln1_bias + d_shift
        large[layer] = (mlp_sum, attention_sum)
        slim[layer] = jnp.concatenate([d_rel.reshape(-1), flat_sum, d_up_bias])
        small[layer] = [d_ln1_gain, d_ln1_bias, d_out_bias, d_ln2_gain, d_ln2_bias, d_down_bias]

    grad_hidden = jnp.concatenate(grads, axis=0)
    mask_grad = jnp.sum(jnp.where(masked, grad_hidden, 0.0), axis=(0, 1))
    grad_input = jnp.where(masked, 0.0, grad_hidden)
    lanes = jnp.concatenate([v for layer in range(LAYERS) for v in small[layer]] + [mask_grad])
    lanes = sum_small(lanes, "tensor", [0, 1])
    slim_size = slim[0].shape[0]
    whole = sum_small(jnp.concatenate(slim + [lanes]), "dp", bits)
    slim_sum = [whole[i * slim_size : (i + 1) * slim_size] for i in range(LAYERS)]
    small_sum = whole[LAYERS * slim_size :].reshape(-1, width)
    local = heads * HEAD_DIM
    rel_size = heads * BUCKETS

    def stacked_small(i):
        return jnp.stack([small_sum[layer * 6 + i] for layer in range(LAYERS)])

    return (
        by_page(result),
        by_page(grad_input),
        small_sum[-1],
        stacked_small(0),
        stacked_small(1),
        jnp.stack(
            [
                jnp.swapaxes(large[i][1][local:].astype(F32).reshape(3, local, width), 1, 2)
                for i in range(LAYERS)
            ]
        ),
        jnp.stack(
            [
                slim_sum[i][rel_size : rel_size + 3 * local].reshape(3, local)[::2]
                for i in range(LAYERS)
            ]
        ),
        jnp.stack([slim_sum[i][:rel_size].reshape(heads, BUCKETS) for i in range(LAYERS)]),
        jnp.stack([large[i][1][:local].astype(F32) for i in range(LAYERS)]),
        stacked_small(2),
        stacked_small(3),
        stacked_small(4),
        jnp.stack([large[i][0][width:].astype(F32) for i in range(LAYERS)]),
        jnp.stack([slim_sum[i][rel_size + 3 * local :] for i in range(LAYERS)]),
        jnp.stack([large[i][0][:width].astype(F32) for i in range(LAYERS)]),
        stacked_small(5),
    )


def solution(mesh):
    placed = (
        P("tensor", "dp", None),
        P("tensor", "dp", None),
        P("tensor", "dp"),
        P(None, "dp"),
        P(),
        P(),
        P(),
        P(),
        P(None, None, None, "tensor"),
        P(None, None, "tensor"),
        P(None, "tensor", None),
        P(None, "tensor", None),
        P(),
        P(),
        P(),
        P(None, None, "tensor"),
        P(None, "tensor"),
        P(None, "tensor", None),
        P(),
    )
    return jax.shard_map(
        functools.partial(shards, mesh.shape["dp"]),
        mesh=mesh,
        in_specs=placed,
        out_specs=(
            P("tensor", "dp", None),
            P("tensor", "dp", None),
            P(),
            P(),
            P(),
            P(None, None, None, "tensor"),
            P(None, None, "tensor"),
            P(None, "tensor", None),
            P(None, "tensor", None),
            P(),
            P(),
            P(),
            P(None, None, "tensor"),
            P(None, "tensor"),
            P(None, "tensor", None),
            P(),
        ),
        check_vma=False,
    )
```

```python
import functools

import jax
import jax.numpy as jnp
from jax import lax
from jax.experimental import pallas as pl
from jax.experimental.pallas import tpu as pltpu
from jax.sharding import PartitionSpec as P

HEAD_DIM = 64
BUCKETS = 732
LAYERS = 2
EPSILON = 1e-06
VMEM_GRANT = 10 * 1024 * 1024
GELU_SCALE = 0.7978845608028654
GELU_CUBE = 0.044715

BF = jnp.bfloat16
F32 = jnp.float32
CORE = [(i, i ^ 1) for i in range(4)]
CHIP = [(i, i ^ 2) for i in range(4)]
VMEM = pl.BlockSpec(memory_space=pltpu.VMEM)
NN = (((1,), (0,)), ((), ()))
NT = (((1,), (1,)), ((), ()))
TN = (((0,), (0,)), ((), ()))


def shape(dims, kind):
    return jax.ShapeDtypeStruct(dims, kind)


def scalar(values):
    return (values, pl.BlockSpec(memory_space=pltpu.SMEM))


def kernel_call(body, name, outs, flops, *operands, scratch=()):
    specs = [x[1] if isinstance(x, tuple) else VMEM for x in operands]
    operands = [x[0] if isinstance(x, tuple) else x for x in operands]
    moved = sum(x.size * x.dtype.itemsize for x in operands) + sum(
        o.size * o.dtype.itemsize for o in outs
    )
    return pl.pallas_call(
        body,
        out_shape=tuple(outs),
        in_specs=specs,
        out_specs=tuple([VMEM] * len(outs)),
        scratch_shapes=list(scratch),
        name=name,
        compiler_params=pltpu.CompilerParams(vmem_limit_bytes=VMEM_GRANT),
        cost_estimate=pl.CostEstimate(flops=flops // 100, bytes_accessed=moved // 100, transcendentals=0),
    )(*operands)


def mxu(left, right, dims):
    return lax.dot_general(left, right, dims, preferred_element_type=F32)


def swap_core(values):
    return lax.ppermute(values, "tensor", CORE)


def swap_chip(values):
    return lax.ppermute(values, "tensor", CHIP)


def tied(values, token):
    return lax.optimization_barrier((values, token))[0]


def spread(own, meanwhile=()):
    far = swap_chip(own)
    near = swap_core(own)
    if meanwhile:
        far = tied(far, meanwhile)
    return [own, near, far, swap_core(far)]


def collect(partial):
    pair_far = partial[2] + swap_core(partial[3])
    return [partial[0], swap_core(partial[1])], swap_chip(pair_far), pair_far


def bias_kernel(table_ref, index_ref, pad_ref, member_ref, out_ref, ordered_ref, bias_ref):
    heads, layers, entries = table_ref.shape
    lanes = 128
    chunks = (entries + lanes - 1) // lanes
    member = member_ref[0]
    low, high = member & 1, member >> 1
    block = index_ref.shape[0] // 4

    def picked(ref, rows, half):
        tile = ref[rows, pl.ds(pl.multiple_of((half ^ high) * lanes, lanes), lanes)]
        return jnp.where(low == 1, jnp.concatenate([tile[:, block:], tile[:, :block]], axis=1), tile)

    for half in range(2):
        columns = slice(half * lanes, half * lanes + lanes)
        pads = picked(pad_ref, slice(None), half)
        bias_ref[:, 0, columns] = jnp.where(pads == 1, -1000000000.0, 0.0)

    def line_of(layer, head, chunk):
        size = min(lanes, entries - chunk * lanes)
        line = table_ref[head, layer : layer + 1, chunk * lanes : chunk * lanes + size].astype(F32)
        return jnp.concatenate([line, jnp.zeros((1, lanes - size), F32)], axis=1) if size < lanes else line

    lines = [[line_of(l, h, c) for c in range(chunks)] for l in range(layers) for h in range(heads)]

    def rows_step(step, carry):
        start = (member ^ (step // 4)) * block + (step % 4) * 16
        rows = pl.ds(pl.multiple_of(start, 16), 16)
        place = pl.ds(pl.multiple_of(step * 16, 16), 16)
        for half in range(2):
            columns = slice(half * lanes, half * lanes + lanes)
            index = picked(index_ref, rows, half)
            ordered_ref[place, columns] = index
            lane, chunk = index & (lanes - 1), index // lanes
            here = [chunk == c for c in range(chunks)]
            for table in range(layers * heads):
                total = jnp.zeros((16, lanes), F32)
                for c in range(chunks):
                    line = jnp.broadcast_to(lines[table][c], (16, lanes))
                    total = jnp.where(here[c], jnp.take_along_axis(line, lane, axis=1), total)
                out_ref[table // heads, table % heads, place, columns] = total.astype(out_ref.dtype)
        return carry

    lax.fori_loop(0, index_ref.shape[0] // 16, rows_step, 0)


def bias_of_buckets(tables, buckets, pads, member):
    heads, layers, entries = tables.shape
    pages, length = pads.shape
    outs = [shape((layers, heads) + buckets.shape, BF), shape(buckets.shape, jnp.int32)]
    outs += [shape((pages, 1, length), F32)]
    return kernel_call(
        bias_kernel, "bias_of_buckets", outs, 4_000_000_000, tables, buckets, pads, scalar(member)
    )


def bucket_kernel(values_ref, index_ref, out_ref):
    heads, size, width = values_ref.shape
    chunk = 32

    def step(i, total):
        start = pl.multiple_of(i * chunk, chunk)
        index = index_ref[pl.ds(start, chunk), :]
        left, right = [], []
        for r in range(chunk):
            row = index[r : r + 1, :]
            at_high = lax.broadcasted_iota(jnp.int32, (24, width), 0) == (row >> 5)
            at_low = lax.broadcasted_iota(jnp.int32, (32, width), 0) == (row & 31)
            right.append(jnp.where(at_low, 1.0, 0.0).astype(BF))
            left.append(
                jnp.concatenate(
                    [
                        jnp.where(at_high, values_ref[h, pl.ds(start + r, 1), :], 0.0).astype(BF)
                        for h in range(heads)
                    ],
                    0,
                )
            )
        return total + mxu(jnp.concatenate(left, 1), jnp.concatenate(right, 1), NT)

    out_ref[...] = lax.fori_loop(0, size // chunk, step, jnp.zeros((heads * 24, 32), F32))


def sum_by_bucket(values, buckets):
    heads = values.shape[0]
    return kernel_call(
        bucket_kernel, "sum_by_bucket", [shape((heads * 24, 32), F32)], 6_000_000_000, values, buckets
    )[0]


def normal_of(values):
    center = values - jnp.mean(values, axis=-1, keepdims=True)
    inverse = lax.rsqrt(jnp.mean(center * center, axis=-1, keepdims=True) + EPSILON)
    return center * inverse, inverse


def of_layer(ref, layer):
    return ref[layer : layer + 1, :].astype(F32)


def mask_columns(masked_ref):
    pages, size = masked_ref.shape
    row = lax.broadcasted_iota(jnp.int32, (size, size), 0)
    diagonal = row == lax.broadcasted_iota(jnp.int32, (size, size), 1)
    flags = masked_ref[...].astype(F32)
    spreads = [jnp.where(diagonal, flags[page : page + 1, :], 0.0) for page in range(pages)]
    return [jnp.sum(values, axis=1, keepdims=True) == 1.0 for values in spreads]


def first_norm_kernel(
    rows_ref, grads_ref, masked_ref, embed_ref, gain_ref, shift_ref, hidden_ref, normed_ref, grad_ref, sums_ref
):
    size, pages, width = rows_ref.shape
    gain, shift = of_layer(gain_ref, 0), of_layer(shift_ref, 0)
    total = jnp.zeros((8, width), F32)
    masks = mask_columns(masked_ref)
    for page in range(pages):
        at = slice(page * size, page * size + size)
        masked = masks[page]
        rows = jnp.where(masked, embed_ref[...].astype(F32), rows_ref[:, page, :].astype(F32))
        hidden_ref[at, :] = rows
        normed_ref[at, :] = (normal_of(rows)[0] * gain + shift).astype(BF)
        grad = grads_ref[:, page, :]
        grad_ref[at, :] = grad
        total = total + fold_rows(grad.astype(F32))
    sums_ref[...] = total


def first_norm(rows, grads, masked, embed, gains, shifts):
    size, pages, width = rows.shape
    flat = (size * pages, width)
    return kernel_call(
        first_norm_kernel,
        "first_norm",
        [shape(flat, F32), shape(flat, BF), shape(flat, BF), shape((8, width), F32)],
        1_000_000_000,
        rows,
        grads,
        masked,
        embed,
        gains,
        shifts,
    )


def norm_kernel(layers, hidden_ref, one_ref, two_ref, three_ref, bias_ref, gain_ref, shift_ref, out_ref, normed_ref):
    size = 64
    bias = of_layer(bias_ref, layers[0])
    gain, shift = of_layer(gain_ref, layers[1]), of_layer(shift_ref, layers[1])

    def step(i, carry):
        at = pl.ds(pl.multiple_of(i * size, size), size)
        total = one_ref[at, :].astype(F32) + two_ref[at, :].astype(F32) + three_ref[at, :].astype(F32)
        rows = hidden_ref[at, :] + total + bias
        out_ref[at, :] = rows
        normed_ref[at, :] = (normal_of(rows)[0] * gain + shift).astype(BF)
        return carry

    lax.fori_loop(0, hidden_ref.shape[0] // size, step, 0, unroll=True)


def add_norm(hidden, terms, layers, biases, gains, shifts):
    return kernel_call(
        functools.partial(norm_kernel, layers),
        "add_norm",
        [shape(hidden.shape, F32), shape(hidden.shape, BF)],
        1_000_000_000,
        hidden,
        *terms,
        biases,
        gains,
        shifts,
    )


def result_kernel(layer, hidden_ref, one_ref, two_ref, three_ref, bias_ref, out_ref):
    size, pages, unused = out_ref.shape
    bias = of_layer(bias_ref, layer)
    for page in range(pages):
        at = slice(page * size, page * size + size)
        total = one_ref[at, :].astype(F32) + two_ref[at, :].astype(F32) + three_ref[at, :].astype(F32)
        out_ref[:, page, :] = (hidden_ref[at, :] + total + bias).astype(BF)


def last_result(hidden, terms, layer, biases, pages):
    rows, width = hidden.shape
    return kernel_call(
        functools.partial(result_kernel, layer),
        "last_result",
        [shape((rows // pages, pages, width), BF)],
        1_000_000_000,
        hidden,
        *terms,
        biases,
    )[0]


def fold_rows(values):
    return jnp.sum(values.reshape(-1, 8, values.shape[-1]), axis=0)


def norm_back_step(at, grad_ref, terms, values_ref, gain, sums_ref):
    total = sum(term[at, :].astype(F32) for term in terms)
    normal, inverse = normal_of(values_ref[at, :])
    scaled = total * gain
    inner = scaled - jnp.mean(scaled, -1, keepdims=True)
    inner = inner - normal * jnp.mean(scaled * normal, -1, keepdims=True)
    grad = grad_ref[at, :].astype(F32) + inner * inverse
    sums_ref[0] += fold_rows(total * normal)
    sums_ref[1] += fold_rows(total)
    return grad


def norm_back_kernel(layer, grad_ref, one_ref, two_ref, three_ref, values_ref, gain_ref, out_ref, low_ref, sums_ref):
    size = 64
    sums_ref[...] = jnp.zeros(sums_ref.shape, F32)

    def step(i, carry):
        at = pl.ds(pl.multiple_of(i * size, size), size)
        terms = (one_ref, two_ref, three_ref)
        grad = norm_back_step(at, grad_ref, terms, values_ref, of_layer(gain_ref, layer), sums_ref)
        sums_ref[2] += fold_rows(grad)
        out_ref[at, :] = grad
        low_ref[at, :] = grad.astype(BF)
        return carry

    lax.fori_loop(0, grad_ref.shape[0] // size, step, 0, unroll=True)


def norm_back(grad, terms, values, layer, gains):
    return kernel_call(
        functools.partial(norm_back_kernel, layer),
        "norm_back",
        [shape(grad.shape, F32), shape(grad.shape, BF), shape((3, 8, grad.shape[-1]), F32)],
        1_500_000_000,
        grad,
        *terms,
        values,
        gains,
    )


def last_norm_back_kernel(
    grad_ref, one_ref, two_ref, three_ref, values_ref, gain_ref, masked_ref, out_ref, sums_ref
):
    size, pages, unused = out_ref.shape
    sums_ref[...] = jnp.zeros(sums_ref.shape, F32)
    masks = mask_columns(masked_ref)
    for page in range(pages):
        at = slice(page * size, page * size + size)
        terms = (one_ref, two_ref, three_ref)
        grad = norm_back_step(at, grad_ref, terms, values_ref, of_layer(gain_ref, 0), sums_ref)
        masked = masks[page]
        sums_ref[2] += fold_rows(jnp.where(masked, grad, 0.0))
        out_ref[:, page, :] = jnp.where(masked, 0.0, grad)


def last_norm_back(grad, terms, values, gains, masked):
    pages, size = masked.shape
    width = grad.shape[-1]
    return kernel_call(
        last_norm_back_kernel,
        "last_norm_back",
        [shape((size, pages, width), F32), shape((3, 8, width), F32)],
        1_500_000_000,
        grad,
        *terms,
        values,
        gains,
        masked,
    )


def page_rows(refs, page, size):
    at = pl.ds(pl.multiple_of(page * size, size), size)
    return jnp.concatenate([ref[at, :] for ref in refs], axis=0)


def put_page(refs, page, size, values):
    at = pl.ds(pl.multiple_of(page * size, size), size)
    for i, ref in enumerate(refs):
        ref[at, :] = values[i * size : (i + 1) * size]


def head_masks(heads, kind):
    lane = lax.broadcasted_iota(jnp.int32, (1, heads * HEAD_DIM), 1)
    return [jnp.where((lane // HEAD_DIM) == h, 1.0, 0.0).astype(kind) for h in range(heads)]


def attention_kernel(
    layer, x0, x1, x2, x3, w_ref, bias_ref, rel_ref, pad_ref, wo_ref, p0, p1, p2, p3, q_ref, k_ref, v_ref, pb_ref, o_ref
):
    pages = pad_ref.shape[0]
    heads = rel_ref.shape[1]
    size = x0.shape[0] // pages

    def step(page, carry):
        masks = head_masks(heads, BF)
        rows = page_rows((x0, x1, x2, x3), page, size)
        q = ((mxu(rows, w_ref[layer, 0], NT) + bias_ref[layer, 0:1, :].astype(F32)) * HEAD_DIM**-0.5).astype(BF)
        k = mxu(rows, w_ref[layer, 1], NT).astype(BF)
        v = (mxu(rows, w_ref[layer, 2], NT) + bias_ref[layer, 1:2, :].astype(F32)).astype(BF)
        q_ref[page], k_ref[page], v_ref[page] = q, k, v
        o = jnp.zeros(q.shape, F32)
        for h in range(heads):
            s = mxu(q * masks[h], k, NT) + (rel_ref[layer, h].astype(F32) + pad_ref[page])
            e = jnp.exp(s - jnp.max(s, axis=-1, keepdims=True))
            pb = (e * (1.0 / jnp.sum(e, axis=-1, keepdims=True))).astype(BF)
            pb_ref[page, h] = pb
            o = o + mxu(pb, v * masks[h], NN)
        o = o.astype(BF)
        o_ref[page] = o
        put_page((p0, p1, p2, p3), page, size, mxu(o, wo_ref[layer], NN).astype(BF))
        return carry

    lax.fori_loop(0, pages, step, 0, unroll=2)


def attention(layer, blocks, w_qkv, qv_bias, rel_bias, pad_bias, w_out):
    pages, unused, length = pad_bias.shape
    heads = rel_bias.shape[1]
    local = heads * HEAD_DIM
    outs = [shape(blocks[0].shape, BF)] * 4 + [shape((pages, length, local), BF)] * 3
    outs += [shape((pages, heads, length, length), BF), shape((pages, length, local), BF)]
    made = kernel_call(
        functools.partial(attention_kernel, layer), "attention", outs, 6_000_000_000, *blocks, w_qkv, qv_bias, rel_bias, pad_bias, w_out
    )
    return made[:4], made[4:]


def attention_back_kernel(
    layer, g0, g1, g2, g3, q_ref, k_ref, v_ref, pb_ref, w_ref, wo_ref, p0, p1, p2, p3, stack_ref, total_ref, sums_ref
):
    pages, heads = pb_ref.shape[:2]
    size = g0.shape[0] // pages
    local = heads * HEAD_DIM
    total_ref[...] = jnp.zeros(total_ref.shape, F32)
    sums_ref[...] = jnp.zeros(sums_ref.shape, F32)

    def step(page, carry):
        masks = head_masks(heads, BF)
        rows = page_rows((g0, g1, g2, g3), page, size)
        go = mxu(rows, wo_ref[layer], NT).astype(BF)
        q, k, v = q_ref[page], k_ref[page], v_ref[page]
        gq = gk = gv = jnp.zeros(q.shape, F32)
        for h in range(heads):
            pb = pb_ref[page, h]
            go_h = go * masks[h]
            gv = gv + mxu(pb, go_h, TN)
            gp = mxu(go_h, v, NT)
            p = pb.astype(F32)
            gs = (p * (gp - jnp.sum(p * gp, axis=-1, keepdims=True))).astype(BF)
            total_ref[h] += gs.astype(F32)
            gq = gq + mxu(gs, k * masks[h], NN)
            gk = gk + mxu(gs, q * masks[h], TN)
        gq = (gq.astype(BF).astype(F32) * HEAD_DIM**-0.5).astype(BF)
        gk, gv = gk.astype(BF), gv.astype(BF)
        stack_ref[page, 0], stack_ref[page, 1], stack_ref[page, 2] = gq, gk, gv
        sums_ref[0] += fold_rows(gq.astype(F32))
        sums_ref[1] += fold_rows(gv.astype(F32))
        ga = mxu(gq, w_ref[layer, 0], NN) + mxu(gk, w_ref[layer, 1], NN) + mxu(gv, w_ref[layer, 2], NN)
        put_page((p0, p1, p2, p3), page, size, ga.astype(BF))
        return carry

    lax.fori_loop(0, pages, step, 0, unroll=2)


def attention_back(layer, blocks, kept, w_qkv, w_out):
    q, k, v, pb, unused = kept
    pages, length, local = q.shape
    heads = pb.shape[1]
    outs = [shape(blocks[0].shape, BF)] * 4
    outs += [shape((pages, 3, length, local), BF), shape((heads, length, length), F32), shape((2, 8, local), F32)]
    made = kernel_call(
        functools.partial(attention_back_kernel, layer), "attention_back", outs, 9_000_000_000, *blocks, q, k, v, pb, w_qkv, w_out
    )
    return made[:4], made[4:]


def fetched(sources, targets, sems):
    copies = [pltpu.make_async_copy(s, t, sems.at[i]) for i, (s, t) in enumerate(zip(sources, targets))]
    for copy in copies:
        copy.start()
    return copies


def fetching_call(body, name, outs, flops, operands, place, scratch):
    moved = sum(x.size * x.dtype.itemsize for x in operands)
    return pl.pallas_call(
        body,
        out_shape=tuple(outs),
        in_specs=[pl.BlockSpec(memory_space=pltpu.HBM)] * len(operands) + [pl.BlockSpec(memory_space=pltpu.SMEM)],
        out_specs=tuple([VMEM] * len(outs)),
        scratch_shapes=[pltpu.VMEM(x.shape, x.dtype) for x in operands]
        + [pltpu.SemaphoreType.DMA((len(operands),))]
        + list(scratch),
        name=name,
        compiler_params=pltpu.CompilerParams(vmem_limit_bytes=2 * VMEM_GRANT),
        cost_estimate=pl.CostEstimate(flops=flops // 100, bytes_accessed=moved // 100, transcendentals=0),
    )(*operands, place)


def attention_grads_kernel(*refs):
    sources, place_ref, keep_ref, send_ref = refs[:10], *refs[10:13]
    targets, sems, acc_ref = refs[13:23], *refs[23:]
    copies = fetched(sources, targets, sems)
    stack_ref, o_ref = targets[8:]
    pages, parts, length, local = stack_ref.shape
    size = targets[0].shape[0] // pages
    acc_ref[...] = jnp.zeros(acc_ref.shape, F32)
    for copy in copies:
        copy.wait()

    def step(page, carry):
        rows = page_rows(targets[:4], page, size)
        grad = page_rows(targets[4:8], page, size)
        acc_ref[:local] += mxu(o_ref[page], grad, TN)
        for t in range(parts):
            acc_ref[(t + 1) * local : (t + 2) * local] += mxu(stack_ref[page, t], rows, TN)
        return carry

    lax.fori_loop(0, pages, step, 0, unroll=2)
    half = keep_ref.shape[0]
    mine = place_ref[0] & 1
    keep_ref[...] = acc_ref[pl.ds(pl.multiple_of(mine * half, half), half), :].astype(BF)
    send_ref[...] = acc_ref[pl.ds(pl.multiple_of((1 - mine) * half, half), half), :].astype(BF)


def attention_grads(rows, grads, stack, o, place):
    local, width = o.shape[-1], rows[0].shape[-1]
    return fetching_call(
        attention_grads_kernel,
        "attention_grads",
        [shape((2 * local, width), BF)] * 2,
        3_000_000_000,
        [*rows, *grads, stack, o],
        place,
        [pltpu.VMEM((4 * local, width), F32)],
    )


def gelu_parts(u):
    square = u * u
    t = jnp.tanh(GELU_SCALE * (u + GELU_CUBE * (square * u)))
    plus = 0.5 * (1.0 + t)
    slope = plus + 0.5 * u * (1.0 - t * t) * (GELU_SCALE * (1.0 + (3.0 * GELU_CUBE) * square))
    return u * plus, slope


def up_rows(layer, at, rows_ref, up_ref, bias_ref, z_ref, slope_ref, block):
    u = mxu(rows_ref[at, :], up_ref[layer], NN) + of_layer(bias_ref, layer)
    z, slope = gelu_parts(u)
    z = z.astype(BF)
    z_ref[block, at, :] = z
    return z, slope


def forward_kernel(layer, c0, c1, c2, c3, up_ref, bias_ref, down_ref, p0, p1, p2, p3, z_ref, slope_ref):
    size = 256
    for block, (rows_ref, out_ref) in enumerate(zip((c0, c1, c2, c3), (p0, p1, p2, p3))):

        def step(i, carry):
            at = pl.ds(pl.multiple_of(i * size, size), size)
            z, slope = up_rows(layer, at, rows_ref, up_ref, bias_ref, z_ref, slope_ref, block)
            slope_ref[block, at, :] = slope.astype(BF)
            out_ref[at, :] = mxu(z, down_ref[layer], NN).astype(BF)
            return carry

        lax.fori_loop(0, rows_ref.shape[0] // size, step, 0)


def feed_forward(layer, blocks, w_up, up_bias, w_down):
    units = w_up.shape[2]
    size = blocks[0].shape[0]
    outs = [shape(blocks[0].shape, BF)] * 4 + [shape((4, size, units), BF)] * 2
    made = kernel_call(functools.partial(forward_kernel, layer), "feed_forward", outs, 4_000_000_000, *blocks, w_up, up_bias, w_down)
    return made[:4], made[4:]


def down_kernel(layer, z_ref, down_ref, p0, p1, p2, p3):
    size = 256
    for block, out_ref in enumerate((p0, p1, p2, p3)):

        def step(i, carry):
            at = pl.ds(pl.multiple_of(i * size, size), size)
            out_ref[at, :] = mxu(z_ref[block, at, :], down_ref[layer], NN).astype(BF)
            return carry

        lax.fori_loop(0, out_ref.shape[0] // size, step, 0)


def down_product(layer, z, w_down):
    outs = [shape((z.shape[1], w_down.shape[2]), BF)] * 4
    return kernel_call(functools.partial(down_kernel, layer), "down_product", outs, 1_500_000_000, z, w_down)


def back_kernel(layer, g0, g1, g2, g3, slope_ref, up_ref, down_ref, p0, p1, p2, p3, gu_ref, sums_ref):
    size = 256
    sums_ref[...] = jnp.zeros(sums_ref.shape, F32)
    for block, (grad_ref, out_ref) in enumerate(zip((g0, g1, g2, g3), (p0, p1, p2, p3))):

        def step(i, carry):
            at = pl.ds(pl.multiple_of(i * size, size), size)
            gz = mxu(grad_ref[at, :], down_ref[layer], NT)
            gu = (gz * slope_ref[block, at, :].astype(F32)).astype(BF)
            gu_ref[block, at, :] = gu
            sums_ref[...] += fold_rows(gu.astype(F32))
            out_ref[at, :] = mxu(gu, up_ref[layer], NT).astype(BF)
            return carry

        lax.fori_loop(0, grad_ref.shape[0] // size, step, 0)


def feed_back(layer, blocks, slope, w_up, w_down):
    size, units = blocks[0].shape[0], w_up.shape[2]
    outs = [shape(blocks[0].shape, BF)] * 4 + [shape((4, size, units), BF), shape((8, units), F32)]
    made = kernel_call(functools.partial(back_kernel, layer), "feed_back", outs, 4_000_000_000, *blocks, slope, w_up, w_down)
    return made[:4], made[4:]


def both_kernel(
    layer, c0, c1, c2, c3, g0, g1, g2, g3, up_ref, bias_ref, down_ref, p0, p1, p2, p3, z_ref, gu_ref, sums_ref
):
    size = 256
    sums_ref[...] = jnp.zeros(sums_ref.shape, F32)
    for block, (rows_ref, grad_ref, out_ref) in enumerate(
        zip((c0, c1, c2, c3), (g0, g1, g2, g3), (p0, p1, p2, p3))
    ):

        def step(i, carry):
            at = pl.ds(pl.multiple_of(i * size, size), size)
            gz = mxu(grad_ref[at, :], down_ref[layer], NT)
            z, slope = up_rows(layer, at, rows_ref, up_ref, bias_ref, z_ref, None, block)
            gu = (gz * slope).astype(BF)
            gu_ref[block, at, :] = gu
            sums_ref[...] += fold_rows(gu.astype(F32))
            out_ref[at, :] = mxu(gu, up_ref[layer], NT).astype(BF)
            return carry

        lax.fori_loop(0, rows_ref.shape[0] // size, step, 0)


def feed_both(layer, blocks, grads, w_up, up_bias, w_down):
    size, units = blocks[0].shape[0], w_up.shape[2]
    outs = [shape(blocks[0].shape, BF)] * 4 + [shape((4, size, units), BF)] * 2 + [shape((8, units), F32)]
    made = kernel_call(
        functools.partial(both_kernel, layer),
        "feed_both",
        outs,
        6_000_000_000,
        *blocks,
        *grads,
        w_up,
        up_bias,
        w_down,
    )
    return made[:4], made[4:]


def feed_grads_kernel(parts, *refs):
    sources, place_ref = refs[:10], refs[10]
    out_refs, refs = refs[11 : 11 + 2 * parts], refs[11 + 2 * parts :]
    targets, sems, both_ref = refs[:10], *refs[10:]
    copies = fetched(sources, targets, sems)
    rows_refs, grad_refs, z_ref, gu_ref = targets[:4], targets[4:8], *targets[8:]
    for copy in copies:
        copy.wait()
    unused, units, width = both_ref.shape
    step = 256
    for start in range(0, units, step):
        rows = slice(start, start + step)
        down = sum(mxu(z_ref[i, :, rows], g[...], TN) for i, g in enumerate(grad_refs))
        both_ref[0, rows, :] = down.astype(BF)
        up = sum(mxu(c[:, rows], gu_ref[i], TN) for i, c in enumerate(rows_refs))
        both_ref[1, rows, :] = up.astype(BF)
    mine = place_ref[0] & 1
    size = units // parts
    for part in range(parts):
        rows = slice(part * size, (part + 1) * size)
        out_refs[2 * part][...] = both_ref[mine, rows, :]
        out_refs[2 * part + 1][...] = both_ref[1 - mine, rows, :]


def feed_grads(rows, grads, z, gu, place, parts):
    units, width = z.shape[-1], rows[0].shape[-1]
    made = fetching_call(
        functools.partial(feed_grads_kernel, parts),
        "feed_grads",
        [shape((units // parts, width), BF)] * (2 * parts),
        4_000_000_000,
        [*rows, *grads, z, gu],
        place,
        [pltpu.VMEM((2, units, width), BF)],
    )
    return [made[2 * i : 2 * i + 2] for i in range(parts)]


def partners(bits, bit):
    return [(i, i ^ (1 << bit)) for i in range(1 << len(bits))]


def halve_kernel(bit, keep_ref, got_ref, place_ref, out_keep_ref, out_send_ref):
    half = out_keep_ref.shape[0]
    mine = (place_ref[0] >> bit) & 1
    for out_ref, which in ((out_send_ref, 1 - mine), (out_keep_ref, mine)):
        at = pl.ds(pl.multiple_of(which * half, half), half)
        out_ref[...] = (keep_ref[at, :].astype(F32) + got_ref[at, :].astype(F32)).astype(BF)


def halve(keep, got, bit, place):
    rows, width = keep.shape
    outs = [shape((rows // 2, width), BF)] * 2
    return kernel_call(
        functools.partial(halve_kernel, bit), "halve", outs, 200_000_000, keep, got, scalar(place)
    )


def join_kernel(bit, own_ref, got_ref, place_ref, out_ref):
    half = own_ref.shape[0]
    mine = (place_ref[0] >> bit) & 1
    out_ref[pl.ds(pl.multiple_of(mine * half, half), half), :] = own_ref[...]
    out_ref[pl.ds(pl.multiple_of((1 - mine) * half, half), half), :] = got_ref[...]


def join(own, got, bit, place):
    rows, width = own.shape
    return kernel_call(
        functools.partial(join_kernel, bit),
        "join",
        [shape((2 * rows, width), BF)],
        200_000_000,
        own,
        got,
        scalar(place),
    )[0]


class PageSum:
    def __init__(self, halves, bits, place):
        self.own, send = halves
        self.bits, self.place = bits, place
        self.cuts = bits[1:3]
        self.plan = [(self.down, bit) for bit in self.cuts] + [(self.turn, None)]
        self.plan += [(self.up, bit) for bit in reversed(self.cuts)]
        self.got = self.swap(send, 0)

    def swap(self, values, bit):
        self.sent = values
        return lax.ppermute(values, "dp", partners(self.bits, bit))

    def down(self, got, bit):
        self.own, send = halve(self.own, got, bit, self.place)
        return self.swap(send, bit)

    def turn(self, got, unused):
        self.own = self.own + got
        for bit in self.bits[3:]:
            self.own = self.own + self.swap(self.own, bit)
        return self.swap(self.own, self.cuts[-1] if self.cuts else 0)

    def up(self, got, bit):
        self.own = join(self.own, got, bit, self.place)
        index = self.bits.index(bit) - 1
        return self.swap(self.own, self.bits[index])

    def step(self, token):
        action, bit = self.plan.pop(0)
        self.got = action(tied(self.got, token), bit)
        return self.sent

    def ended(self):
        return self.own, self.got


def sum_small(values, axis, bits, count):
    for bit in bits:
        values = values + lax.ppermute(values, axis, partners(range(count), bit))
    return values


def row_sum(values):
    return jnp.sum(values, axis=0, keepdims=True)


def pack_rows_kernel(ones0, twos0, ones1, twos1, last_ref, out_ref):
    out_ref[...] = jnp.zeros(out_ref.shape, F32)
    for layer, (one_ref, two_ref) in enumerate(((ones0, twos0), (ones1, twos1))):
        down = ones1[2] if layer == 0 else last_ref[...]
        members = [one_ref[0], one_ref[1], two_ref[2], two_ref[0], two_ref[1], down]
        for i, member in enumerate(members):
            out_ref[2 * i + layer : 2 * i + layer + 1, :] = row_sum(member)
    out_ref[12:13, :] = row_sum(ones0[2])


def pack_rows(ones, twos, last):
    return kernel_call(
        pack_rows_kernel,
        "pack_rows",
        [shape((16, last.shape[-1]), F32)],
        1_000_000,
        ones[0],
        twos[0],
        ones[1],
        twos[1],
        last,
    )[0]


def pack_all_kernel(rows_ref, qv0, qv1, up0, up1, rel0, rel1, out_ref):
    local = qv0.shape[-1]
    out_ref[:16, :] = rows_ref[...]
    out_ref[16:, :] = jnp.zeros((32, out_ref.shape[1]), F32)
    for layer, (qv_ref, up_ref, rel_ref) in enumerate(((qv0, up0, rel0), (qv1, up1, rel1))):
        out_ref[16 + layer : 17 + layer, :] = row_sum(up_ref[...])
        for i in range(2):
            out_ref[18 + 2 * layer + i : 19 + 2 * layer + i, :local] = row_sum(qv_ref[i])
        heads = rel_ref.shape[0] // 24
        for h in range(heads):
            start = (layer * heads + h) * 128
            out_ref[24:48, start : start + 32] = rel_ref[h * 24 : h * 24 + 24, :]


def pack_all(rows, qv_sums, up_sums, rel_sums):
    return kernel_call(
        pack_all_kernel,
        "pack_all",
        [shape((48, rows.shape[-1]), F32)],
        1_000_000,
        rows,
        *qv_sums,
        *up_sums,
        *rel_sums,
    )[0]


def unpack_kernel(all_ref, *out_refs):
    rows, mask_ref, up_ref, qv_ref, rel_ref = out_refs[:6], *out_refs[6:]
    for i, row_ref in enumerate(rows):
        row_ref[...] = all_ref[2 * i : 2 * i + 2, :]
    mask_ref[...] = all_ref[12:13, :]
    up_ref[...] = all_ref[16:18, :]
    heads, layers, entries = rel_ref.shape
    local = qv_ref.shape[-1]
    for layer in range(layers):
        qv_ref[layer] = all_ref[18 + 2 * layer : 20 + 2 * layer, :local]
        for h in range(heads):
            start = (layer * heads + h) * 128
            for j in range(6):
                lines = [all_ref[24 + 4 * j + r : 25 + 4 * j + r, start : start + 32] for r in range(4)]
                size = min(128, entries - 128 * j)
                line = jnp.concatenate(lines, axis=1)[:, :size]
                rel_ref[h, layer : layer + 1, 128 * j : 128 * j + size] = line


def unpack(values, heads, entries):
    width = values.shape[-1]
    outs = [shape((LAYERS, width), F32)] * 6 + [shape((1, width), F32), shape((LAYERS, width), F32)]
    outs += [shape((LAYERS, 2, heads * HEAD_DIM), F32), shape((heads, LAYERS, entries), F32)]
    return kernel_call(unpack_kernel, "unpack", outs, 1_000_000, values)


def assemble_kernel(layer, pieces, own_ref, got_ref, place_ref, *refs):
    out_refs, (stage_ref, sems) = refs[-2 - len(pieces) : -2], refs[-2:]
    half = own_ref.shape[0]
    mine = place_ref[0] & 1
    stage_ref[pl.ds(pl.multiple_of(mine * half, half), half), :] = own_ref[...].astype(F32)
    stage_ref[pl.ds(pl.multiple_of((1 - mine) * half, half), half), :] = got_ref[...].astype(F32)
    copies = []
    for out_ref, parts in zip(out_refs, pieces):
        for index, start, rows in parts:
            target = out_ref.at[(layer,) + index]
            source = stage_ref.at[pl.ds(start, rows), :]
            copies.append(pltpu.make_async_copy(source, target, sems.at[len(copies)]))
    for copy in copies:
        copy.start()
    for copy in copies:
        copy.wait()


def assemble(layer, name, pieces, outs, own, got, place, before):
    rows, width = own.shape
    anywhere = pl.BlockSpec(memory_space=pl.ANY)
    count = sum(len(parts) for parts in pieces)
    return pl.pallas_call(
        functools.partial(assemble_kernel, layer, pieces),
        out_shape=tuple(outs),
        in_specs=[VMEM, VMEM, pl.BlockSpec(memory_space=pltpu.SMEM)] + [anywhere] * len(before),
        out_specs=tuple([anywhere] * len(outs)),
        scratch_shapes=[pltpu.VMEM((2 * rows, width), F32), pltpu.SemaphoreType.DMA((count,))],
        input_output_aliases={3 + i: i for i in range(len(before))},
        name=name,
        compiler_params=pltpu.CompilerParams(vmem_limit_bytes=VMEM_GRANT),
        cost_estimate=pl.CostEstimate(flops=1_000_000, bytes_accessed=rows * width, transcendentals=0),
    )(own, got, place, *before)


def assemble_feed(layer, part, parts, sums, place, before=()):
    own, got = sums.ended()
    size, width = own.shape
    pieces = [[((pl.ds(part * size, size),), 0, size)], [((pl.ds(part * size, size),), size, size)]]
    outs = [shape((LAYERS, parts * size, width), F32)] * 2
    return assemble(layer, "assemble_feed", pieces, outs, own, got, place, before)


def assemble_attention(layer, sums, place, before=()):
    own, got = sums.ended()
    local, width = own.shape[0] // 2, own.shape[1]
    pieces = [[((), 0, local)], [((t,), (t + 1) * local, local) for t in range(3)]]
    outs = [shape((LAYERS, local, width), F32), shape((LAYERS, 3, local, width), F32)]
    return assemble(layer, "assemble_attention", pieces, outs, own, got, place, before)


def shards(
    n_dp,
    patch_rows,
    cotangent,
    mask_flags,
    pad_flags,
    buckets,
    mask_emb,
    ln1_gain,
    ln1_bias,
    w_qkv,
    qv_bias,
    rel_table,
    w_out,
    out_bias,
    ln2_gain,
    ln2_bias,
    w_up,
    up_bias,
    w_down,
    down_bias,
):
    member = lax.axis_index("tensor").reshape(1).astype(jnp.int32)
    place = lax.axis_index("dp").reshape(1).astype(jnp.int32)
    bits = list(range(n_dp.bit_length() - 1))
    pages = patch_rows.shape[1]
    heads, entries = rel_table.shape[1:]
    last = LAYERS - 1
    masked = mask_flags.T
    w_qkv = jnp.swapaxes(w_qkv, 2, 3)

    hidden, own, last_own, last_sum = first_norm(
        patch_rows, cotangent, masked, mask_emb.reshape(1, -1), ln1_gain, ln1_bias
    )
    rel_bias, ordered, pad_bias = bias_of_buckets(jnp.swapaxes(rel_table, 0, 1), buckets, pad_flags.T, member)
    blocks = spread(own, (rel_bias,))
    last_blocks = spread(tied(last_own, blocks[3]))

    kept = []
    for layer in range(LAYERS):
        rows_one, before = blocks, hidden
        partial, saved = attention(layer, rows_one, w_qkv, qv_bias, rel_bias, pad_bias, w_out)
        near, far, unused = collect(partial)
        middle, own = add_norm(hidden, near + [far], (layer, layer), out_bias, ln2_gain, ln2_bias)
        rows_two = spread(own)
        if layer == last:
            partial, (z, gu, up_sums) = feed_both(layer, rows_two, last_blocks, w_up, up_bias, w_down)
            kept.append((rows_one, before, saved, middle, rows_two, z, gu))
        else:
            partial, (z, slope) = feed_forward(layer, rows_two, w_up, up_bias, w_down)
            kept.append((rows_one, before, saved, middle, rows_two, z, slope))
            near, far, unused = collect(partial)
            hidden, own = add_norm(middle, near + [far], (layer, layer + 1), down_bias, ln1_gain, ln1_bias)
            blocks = spread(own)

    rows_one, before, saved, middle, rows_two, z, gu = kept[last]
    near, far, sent = collect(partial)
    mlp = feed_grads(rows_two, last_blocks, tied(z, sent), gu, place, 1)
    mlp1 = PageSum(mlp[0], bits, place)
    far = tied(far, mlp)
    g1, low, twos1 = norm_back(last_own, near + [far], middle, last, ln2_gain)
    result_parts = down_product(last, tied(z, low), w_down)
    out_blocks = spread(low, result_parts)
    partial, (stack, totals, qv1) = attention_back(last, out_blocks, saved, w_qkv, w_out)
    near, far, sent = collect(partial)
    mix = attention_grads(rows_one, out_blocks, tied(stack, sent), saved[-1], place)
    mix1 = PageSum(mix, bits, place)
    far = tied(far, mlp1.step(mix))
    grad, low, ones1 = norm_back(g1, near + [far], before, last, ln1_gain)
    rel1 = sum_by_bucket(tied(totals, low), ordered)
    token = mlp1.step(rel1)
    grad_blocks = spread(low, (token,))
    up1 = up_sums

    rows_one, before, saved, middle, rows_two, z, slope = kept[0]
    partial, (gu, up0) = feed_back(0, grad_blocks, slope, w_up, w_down)
    near, far, sent = collect(partial)
    mlp = feed_grads(rows_two, grad_blocks, tied(z, sent), gu, place, 2)
    mlp0a = PageSum(mlp[0], bits, place)
    token = mix1.step(mlp)
    token = mlp1.step(token)
    far = tied(far, token)
    g1, low, twos0 = norm_back(grad, near + [far], middle, 0, ln2_gain)
    token = mix1.step(low)
    token = mlp1.step(token)
    token = mlp0a.step(token)
    mlp0b = PageSum([mlp[1][0], tied(mlp[1][1], token)], bits, place)
    out_blocks = spread(low, (token,))
    result_near, result_far, unused = collect([tied(p, out_blocks[3]) for p in result_parts])
    partial, (stack, totals, qv0) = attention_back(0, out_blocks, saved, w_qkv, w_out)
    near, far, sent = collect(partial)
    mix = attention_grads(rows_one, out_blocks, tied(stack, sent), saved[-1], place)
    mix0 = PageSum(mix, bits, place)
    token = mlp0a.step(mix)
    token = mlp0b.step(token)
    token = mix1.step(token)
    token = mlp1.step(token)
    far = tied(far, token)
    grad, ones0 = last_norm_back(g1, near + [far], before, ln1_gain, masked)

    rows = pack_rows((ones0, ones1), (twos0, twos1), last_sum)
    rows = rows + swap_core(rows)
    rel0 = sum_by_bucket(tied(totals, rows), ordered)
    token = mlp0a.step(rel0)
    token = mix0.step(token)
    token = mlp0b.step(token)
    rows = rows + swap_chip(tied(rows, rel0))
    small = pack_all(tied(rows, token), (qv0, qv1), (up0, up1), (rel0, rel1))
    small_got = lax.ppermute(small, "dp", partners(bits, 0))
    token = mix1.step(small)
    result = last_result(kept[last][3], result_near + [tied(result_far, token)], last, down_bias, pages)
    token = mlp0a.step((token, result))
    token = mix0.step(token)
    token = mlp0b.step(token)
    token = mix1.step(token)
    small = small + tied(small_got, token)
    small_got = lax.ppermute(small, "dp", partners(bits, bits[1])) if len(bits) > 1 else 0.0
    token = mlp0a.step((token, small))
    d_mlp = assemble_feed(last, 0, 1, mlp1, tied(place, token))
    token = mix0.step((token, d_mlp))
    token = mlp0b.step(token)
    small = sum_small(small + tied(small_got, token), "dp", bits[2:], len(bits))
    d_mix = assemble_attention(last, mix1, tied(place, token))
    token = mix0.step((token, d_mix))
    token = mlp0b.step(token)
    d_mlp = assemble_feed(0, 0, 2, mlp0a, tied(place, token), d_mlp)
    token = mix0.step((token, d_mlp))
    d_mlp = assemble_feed(0, 1, 2, mlp0b, tied(place, token), d_mlp)
    d_mix = assemble_attention(0, mix0, tied(place, token), d_mix)
    small = unpack(small, heads, entries)
    d_ln1_gain, d_ln1_bias, d_out_bias, d_ln2_gain, d_ln2_bias, d_down_bias, d_mask, d_up_bias, d_qv, d_rel = small
    return (
        result,
        grad,
        d_mask.reshape(-1),
        d_ln1_gain,
        d_ln1_bias,
        jnp.swapaxes(d_mix[1], 2, 3),
        d_qv,
        jnp.swapaxes(d_rel, 0, 1),
        d_mix[0],
        d_out_bias,
        d_ln2_gain,
        d_ln2_bias,
        d_mlp[1],
        d_up_bias,
        d_mlp[0],
        d_down_bias,
    )


def solution(mesh):
    rows = P("tensor", "dp", None)
    units = P(None, "tensor", None)
    columns = P(None, None, "tensor")
    whole = P()
    return jax.shard_map(
        functools.partial(shards, mesh.shape["dp"]),
        mesh=mesh,
        in_specs=(
            rows,
            rows,
            P("tensor", "dp"),
            P(None, "dp"),
            whole,
            whole,
            whole,
            whole,
            P(None, None, None, "tensor"),
            columns,
            units,
            units,
            whole,
            whole,
            whole,
            columns,
            P(None, "tensor"),
            units,
            whole,
        ),
        out_specs=(
            rows,
            rows,
            whole,
            whole,
            whole,
            P(None, None, None, "tensor"),
            columns,
            units,
            units,
            whole,
            whole,
            whole,
            columns,
            P(None, "tensor"),
            units,
            whole,
        ),
        check_vma=False,
    )
```

```python
import functools

import jax
import jax.numpy as jnp
from jax import lax
from jax.experimental import pallas as pl
from jax.experimental.pallas import tpu as pltpu
from jax.sharding import PartitionSpec as P

HEAD_DIM = 64
BUCKETS = 732
LAYERS = 2
EPSILON = 1e-06
VMEM_GRANT = 10 * 1024 * 1024
GELU_SCALE = 0.7978845608028654
GELU_CUBE = 0.044715

BF = jnp.bfloat16
F32 = jnp.float32
CORE = [(i, i ^ 1) for i in range(4)]
CHIP = [(i, i ^ 2) for i in range(4)]
VMEM = pl.BlockSpec(memory_space=pltpu.VMEM)
NN = (((1,), (0,)), ((), ()))
NT = (((1,), (1,)), ((), ()))
TN = (((0,), (0,)), ((), ()))


def shape(dims, kind):
    return jax.ShapeDtypeStruct(dims, kind)


def scalar(values):
    return (values, pl.BlockSpec(memory_space=pltpu.SMEM))


def kernel_call(body, name, outs, flops, *operands, scratch=()):
    specs = [x[1] if isinstance(x, tuple) else VMEM for x in operands]
    operands = [x[0] if isinstance(x, tuple) else x for x in operands]
    moved = sum(x.size * x.dtype.itemsize for x in operands) + sum(
        o.size * o.dtype.itemsize for o in outs
    )
    return pl.pallas_call(
        body,
        out_shape=tuple(outs),
        in_specs=specs,
        out_specs=tuple([VMEM] * len(outs)),
        scratch_shapes=list(scratch),
        name=name,
        compiler_params=pltpu.CompilerParams(vmem_limit_bytes=VMEM_GRANT),
        cost_estimate=pl.CostEstimate(flops=flops // 100, bytes_accessed=moved // 100, transcendentals=0),
    )(*operands)


def mxu(left, right, dims):
    return lax.dot_general(left, right, dims, preferred_element_type=F32)


def swap_core(values):
    return lax.ppermute(values, "tensor", CORE)


def swap_chip(values):
    return lax.ppermute(values, "tensor", CHIP)


def tied(values, token):
    return lax.optimization_barrier((values, token))[0]


def spread(own, meanwhile=()):
    far = swap_chip(own)
    near = swap_core(own)
    if meanwhile:
        far = tied(far, meanwhile)
    return [own, near, far, swap_core(far)]


def collect(partial):
    pair_far = partial[2] + swap_core(partial[3])
    return [partial[0], swap_core(partial[1])], swap_chip(pair_far), pair_far


def bias_kernel(table_ref, index_ref, pad_ref, member_ref, out_ref, ordered_ref, bias_ref):
    heads, layers, entries = table_ref.shape
    lanes = 128
    chunks = (entries + lanes - 1) // lanes
    member = member_ref[0]
    low, high = member & 1, member >> 1
    block = index_ref.shape[0] // 4

    def picked(ref, rows, half):
        tile = ref[rows, pl.ds(pl.multiple_of((half ^ high) * lanes, lanes), lanes)]
        return jnp.where(low == 1, jnp.concatenate([tile[:, block:], tile[:, :block]], axis=1), tile)

    for half in range(2):
        columns = slice(half * lanes, half * lanes + lanes)
        pads = picked(pad_ref, slice(None), half)
        bias_ref[:, 0, columns] = jnp.where(pads == 1, -1000000000.0, 0.0)

    def line_of(layer, head, chunk):
        size = min(lanes, entries - chunk * lanes)
        line = table_ref[head, layer : layer + 1, chunk * lanes : chunk * lanes + size].astype(F32)
        return jnp.concatenate([line, jnp.zeros((1, lanes - size), F32)], axis=1) if size < lanes else line

    lines = [[line_of(l, h, c) for c in range(chunks)] for l in range(layers) for h in range(heads)]

    def rows_step(step, carry):
        start = (member ^ (step // 4)) * block + (step % 4) * 16
        rows = pl.ds(pl.multiple_of(start, 16), 16)
        place = pl.ds(pl.multiple_of(step * 16, 16), 16)
        for half in range(2):
            columns = slice(half * lanes, half * lanes + lanes)
            index = picked(index_ref, rows, half)
            ordered_ref[place, columns] = index
            lane, chunk = index & (lanes - 1), index // lanes
            here = [chunk == c for c in range(chunks)]
            for table in range(layers * heads):
                total = jnp.zeros((16, lanes), F32)
                for c in range(chunks):
                    line = jnp.broadcast_to(lines[table][c], (16, lanes))
                    total = jnp.where(here[c], jnp.take_along_axis(line, lane, axis=1), total)
                out_ref[table // heads, table % heads, place, columns] = total.astype(out_ref.dtype)
        return carry

    lax.fori_loop(0, index_ref.shape[0] // 16, rows_step, 0)


def bias_of_buckets(tables, buckets, pads, member):
    heads, layers, entries = tables.shape
    pages, length = pads.shape
    outs = [shape((layers, heads) + buckets.shape, BF), shape(buckets.shape, jnp.int32)]
    outs += [shape((pages, 1, length), F32)]
    return kernel_call(
        bias_kernel, "bias_of_buckets", outs, 4_000_000_000, tables, buckets, pads, scalar(member)
    )


def bucket_kernel(values_ref, index_ref, out_ref):
    heads, size, width = values_ref.shape
    chunk = 32

    def step(i, total):
        start = pl.multiple_of(i * chunk, chunk)
        index = index_ref[pl.ds(start, chunk), :]
        left, right = [], []
        for r in range(chunk):
            row = index[r : r + 1, :]
            at_high = lax.broadcasted_iota(jnp.int32, (24, width), 0) == (row >> 5)
            at_low = lax.broadcasted_iota(jnp.int32, (32, width), 0) == (row & 31)
            right.append(jnp.where(at_low, 1.0, 0.0).astype(BF))
            left.append(
                jnp.concatenate(
                    [
                        jnp.where(at_high, values_ref[h, pl.ds(start + r, 1), :], 0.0).astype(BF)
                        for h in range(heads)
                    ],
                    0,
                )
            )
        return total + mxu(jnp.concatenate(left, 1), jnp.concatenate(right, 1), NT)

    out_ref[...] = lax.fori_loop(0, size // chunk, step, jnp.zeros((heads * 24, 32), F32))


def sum_by_bucket(values, buckets):
    heads = values.shape[0]
    return kernel_call(
        bucket_kernel, "sum_by_bucket", [shape((heads * 24, 32), F32)], 6_000_000_000, values, buckets
    )[0]


def normal_of(values):
    center = values - jnp.mean(values, axis=-1, keepdims=True)
    inverse = lax.rsqrt(jnp.mean(center * center, axis=-1, keepdims=True) + EPSILON)
    return center * inverse, inverse


def of_layer(ref, layer):
    return ref[layer : layer + 1, :].astype(F32)


def mask_columns(masked_ref):
    pages, size = masked_ref.shape
    row = lax.broadcasted_iota(jnp.int32, (size, size), 0)
    diagonal = row == lax.broadcasted_iota(jnp.int32, (size, size), 1)
    flags = masked_ref[...].astype(F32)
    spreads = [jnp.where(diagonal, flags[page : page + 1, :], 0.0) for page in range(pages)]
    return [jnp.sum(values, axis=1, keepdims=True) == 1.0 for values in spreads]


def first_norm_kernel(
    rows_ref, grads_ref, masked_ref, embed_ref, gain_ref, shift_ref, hidden_ref, normed_ref, grad_ref, sums_ref
):
    size, pages, width = rows_ref.shape
    gain, shift = of_layer(gain_ref, 0), of_layer(shift_ref, 0)
    total = jnp.zeros((8, width), F32)
    masks = mask_columns(masked_ref)
    for page in range(pages):
        at = slice(page * size, page * size + size)
        masked = masks[page]
        rows = jnp.where(masked, embed_ref[...].astype(F32), rows_ref[:, page, :].astype(F32))
        hidden_ref[at, :] = rows
        normed_ref[at, :] = (normal_of(rows)[0] * gain + shift).astype(BF)
        grad = grads_ref[:, page, :]
        grad_ref[at, :] = grad
        total = total + fold_rows(grad.astype(F32))
    sums_ref[...] = total


def first_norm(rows, grads, masked, embed, gains, shifts):
    size, pages, width = rows.shape
    flat = (size * pages, width)
    return kernel_call(
        first_norm_kernel,
        "first_norm",
        [shape(flat, F32), shape(flat, BF), shape(flat, BF), shape((8, width), F32)],
        1_000_000_000,
        rows,
        grads,
        masked,
        embed,
        gains,
        shifts,
    )


def norm_kernel(layers, hidden_ref, one_ref, two_ref, three_ref, bias_ref, gain_ref, shift_ref, out_ref, normed_ref):
    size = 64
    bias = of_layer(bias_ref, layers[0])
    gain, shift = of_layer(gain_ref, layers[1]), of_layer(shift_ref, layers[1])

    def step(i, carry):
        at = pl.ds(pl.multiple_of(i * size, size), size)
        total = one_ref[at, :].astype(F32) + two_ref[at, :].astype(F32) + three_ref[at, :].astype(F32)
        rows = hidden_ref[at, :] + total + bias
        out_ref[at, :] = rows
        normed_ref[at, :] = (normal_of(rows)[0] * gain + shift).astype(BF)
        return carry

    lax.fori_loop(0, hidden_ref.shape[0] // size, step, 0, unroll=True)


def add_norm(hidden, terms, layers, biases, gains, shifts):
    return kernel_call(
        functools.partial(norm_kernel, layers),
        "add_norm",
        [shape(hidden.shape, F32), shape(hidden.shape, BF)],
        1_000_000_000,
        hidden,
        *terms,
        biases,
        gains,
        shifts,
    )


def result_kernel(layer, hidden_ref, one_ref, two_ref, three_ref, bias_ref, out_ref):
    size, pages, unused = out_ref.shape
    bias = of_layer(bias_ref, layer)
    for page in range(pages):
        at = slice(page * size, page * size + size)
        total = one_ref[at, :].astype(F32) + two_ref[at, :].astype(F32) + three_ref[at, :].astype(F32)
        out_ref[:, page, :] = (hidden_ref[at, :] + total + bias).astype(BF)


def last_result(hidden, terms, layer, biases, pages):
    rows, width = hidden.shape
    return kernel_call(
        functools.partial(result_kernel, layer),
        "last_result",
        [shape((rows // pages, pages, width), BF)],
        1_000_000_000,
        hidden,
        *terms,
        biases,
    )[0]


def fold_rows(values):
    return jnp.sum(values.reshape(-1, 8, values.shape[-1]), axis=0)


def norm_back_step(at, grad_ref, terms, values_ref, gain, sums_ref):
    total = sum(term[at, :].astype(F32) for term in terms)
    normal, inverse = normal_of(values_ref[at, :])
    scaled = total * gain
    inner = scaled - jnp.mean(scaled, -1, keepdims=True)
    inner = inner - normal * jnp.mean(scaled * normal, -1, keepdims=True)
    grad = grad_ref[at, :].astype(F32) + inner * inverse
    sums_ref[0] += fold_rows(total * normal)
    sums_ref[1] += fold_rows(total)
    return grad


def norm_back_kernel(layer, grad_ref, one_ref, two_ref, three_ref, values_ref, gain_ref, out_ref, low_ref, sums_ref):
    size = 64
    sums_ref[...] = jnp.zeros(sums_ref.shape, F32)

    def step(i, carry):
        at = pl.ds(pl.multiple_of(i * size, size), size)
        terms = (one_ref, two_ref, three_ref)
        grad = norm_back_step(at, grad_ref, terms, values_ref, of_layer(gain_ref, layer), sums_ref)
        sums_ref[2] += fold_rows(grad)
        out_ref[at, :] = grad
        low_ref[at, :] = grad.astype(BF)
        return carry

    lax.fori_loop(0, grad_ref.shape[0] // size, step, 0, unroll=True)


def norm_back(grad, terms, values, layer, gains):
    return kernel_call(
        functools.partial(norm_back_kernel, layer),
        "norm_back",
        [shape(grad.shape, F32), shape(grad.shape, BF), shape((3, 8, grad.shape[-1]), F32)],
        1_500_000_000,
        grad,
        *terms,
        values,
        gains,
    )


def last_norm_back_kernel(
    grad_ref, one_ref, two_ref, three_ref, values_ref, gain_ref, masked_ref, out_ref, sums_ref
):
    size, pages, unused = out_ref.shape
    sums_ref[...] = jnp.zeros(sums_ref.shape, F32)
    masks = mask_columns(masked_ref)
    for page in range(pages):
        at = slice(page * size, page * size + size)
        terms = (one_ref, two_ref, three_ref)
        grad = norm_back_step(at, grad_ref, terms, values_ref, of_layer(gain_ref, 0), sums_ref)
        masked = masks[page]
        sums_ref[2] += fold_rows(jnp.where(masked, grad, 0.0))
        out_ref[:, page, :] = jnp.where(masked, 0.0, grad)


def last_norm_back(grad, terms, values, gains, masked):
    pages, size = masked.shape
    width = grad.shape[-1]
    return kernel_call(
        last_norm_back_kernel,
        "last_norm_back",
        [shape((size, pages, width), F32), shape((3, 8, width), F32)],
        1_500_000_000,
        grad,
        *terms,
        values,
        gains,
        masked,
    )


def page_rows(refs, page, size):
    at = pl.ds(pl.multiple_of(page * size, size), size)
    return jnp.concatenate([ref[at, :] for ref in refs], axis=0)


def put_page(refs, page, size, values):
    at = pl.ds(pl.multiple_of(page * size, size), size)
    for i, ref in enumerate(refs):
        ref[at, :] = values[i * size : (i + 1) * size]


def head_masks(heads, kind):
    lane = lax.broadcasted_iota(jnp.int32, (1, heads * HEAD_DIM), 1)
    return [jnp.where((lane // HEAD_DIM) == h, 1.0, 0.0).astype(kind) for h in range(heads)]


def attention_kernel(
    layer, x0, x1, x2, x3, w_ref, bias_ref, rel_ref, pad_ref, wo_ref, p0, p1, p2, p3, q_ref, k_ref, v_ref, pb_ref, o_ref
):
    pages = pad_ref.shape[0]
    heads = rel_ref.shape[1]
    size = x0.shape[0] // pages

    def step(page, carry):
        masks = head_masks(heads, BF)
        rows = page_rows((x0, x1, x2, x3), page, size)
        q = ((mxu(rows, w_ref[layer, 0], NT) + bias_ref[layer, 0:1, :].astype(F32)) * HEAD_DIM**-0.5).astype(BF)
        k = mxu(rows, w_ref[layer, 1], NT).astype(BF)
        v = (mxu(rows, w_ref[layer, 2], NT) + bias_ref[layer, 1:2, :].astype(F32)).astype(BF)
        q_ref[page], k_ref[page], v_ref[page] = q, k, v
        o = jnp.zeros(q.shape, F32)
        for h in range(heads):
            s = mxu(q * masks[h], k, NT) + (rel_ref[layer, h].astype(F32) + pad_ref[page])
            e = jnp.exp(s - jnp.max(s, axis=-1, keepdims=True))
            pb = (e * (1.0 / jnp.sum(e, axis=-1, keepdims=True))).astype(BF)
            pb_ref[page, h] = pb
            o = o + mxu(pb, v * masks[h], NN)
        o = o.astype(BF)
        o_ref[page] = o
        put_page((p0, p1, p2, p3), page, size, mxu(o, wo_ref[layer], NN).astype(BF))
        return carry

    lax.fori_loop(0, pages, step, 0, unroll=2)


def attention(layer, blocks, w_qkv, qv_bias, rel_bias, pad_bias, w_out):
    pages, unused, length = pad_bias.shape
    heads = rel_bias.shape[1]
    local = heads * HEAD_DIM
    outs = [shape(blocks[0].shape, BF)] * 4 + [shape((pages, length, local), BF)] * 3
    outs += [shape((pages, heads, length, length), BF), shape((pages, length, local), BF)]
    made = kernel_call(
        functools.partial(attention_kernel, layer), "attention", outs, 6_000_000_000, *blocks, w_qkv, qv_bias, rel_bias, pad_bias, w_out
    )
    return made[:4], made[4:]


def attention_back_kernel(
    layer, g0, g1, g2, g3, q_ref, k_ref, v_ref, pb_ref, w_ref, wo_ref, p0, p1, p2, p3, stack_ref, total_ref, sums_ref
):
    pages, heads = pb_ref.shape[:2]
    size = g0.shape[0] // pages
    local = heads * HEAD_DIM
    total_ref[...] = jnp.zeros(total_ref.shape, F32)
    sums_ref[...] = jnp.zeros(sums_ref.shape, F32)

    def step(page, carry):
        masks = head_masks(heads, BF)
        rows = page_rows((g0, g1, g2, g3), page, size)
        go = mxu(rows, wo_ref[layer], NT).astype(BF)
        q, k, v = q_ref[page], k_ref[page], v_ref[page]
        gq = gk = gv = jnp.zeros(q.shape, F32)
        for h in range(heads):
            pb = pb_ref[page, h]
            go_h = go * masks[h]
            gv = gv + mxu(pb, go_h, TN)
            gp = mxu(go_h, v, NT)
            p = pb.astype(F32)
            gs = (p * (gp - jnp.sum(p * gp, axis=-1, keepdims=True))).astype(BF)
            total_ref[h] += gs.astype(F32)
            gq = gq + mxu(gs, k * masks[h], NN)
            gk = gk + mxu(gs, q * masks[h], TN)
        gq = (gq.astype(BF).astype(F32) * HEAD_DIM**-0.5).astype(BF)
        gk, gv = gk.astype(BF), gv.astype(BF)
        stack_ref[page, 0], stack_ref[page, 1], stack_ref[page, 2] = gq, gk, gv
        sums_ref[0] += fold_rows(gq.astype(F32))
        sums_ref[1] += fold_rows(gv.astype(F32))
        ga = mxu(gq, w_ref[layer, 0], NN) + mxu(gk, w_ref[layer, 1], NN) + mxu(gv, w_ref[layer, 2], NN)
        put_page((p0, p1, p2, p3), page, size, ga.astype(BF))
        return carry

    lax.fori_loop(0, pages, step, 0, unroll=2)


def attention_back(layer, blocks, kept, w_qkv, w_out):
    q, k, v, pb, unused = kept
    pages, length, local = q.shape
    heads = pb.shape[1]
    outs = [shape(blocks[0].shape, BF)] * 4
    outs += [shape((pages, 3, length, local), BF), shape((heads, length, length), F32), shape((2, 8, local), F32)]
    made = kernel_call(
        functools.partial(attention_back_kernel, layer), "attention_back", outs, 9_000_000_000, *blocks, q, k, v, pb, w_qkv, w_out
    )
    return made[:4], made[4:]


def attention_grads_kernel(*refs):
    rows_refs, grad_refs, (stack_ref, o_ref, place_ref, keep_ref, send_ref, acc_ref) = refs[:4], refs[4:8], refs[8:]
    pages, parts, length, local = stack_ref.shape
    size = rows_refs[0].shape[0] // pages
    acc_ref[...] = jnp.zeros(acc_ref.shape, F32)

    def step(page, carry):
        rows = page_rows(rows_refs, page, size)
        grad = page_rows(grad_refs, page, size)
        acc_ref[:local] += mxu(o_ref[page], grad, TN)
        for t in range(parts):
            acc_ref[(t + 1) * local : (t + 2) * local] += mxu(stack_ref[page, t], rows, TN)
        return carry

    lax.fori_loop(0, pages, step, 0, unroll=2)
    half = keep_ref.shape[0]
    mine = place_ref[0] & 1
    keep_ref[...] = acc_ref[pl.ds(pl.multiple_of(mine * half, half), half), :].astype(BF)
    send_ref[...] = acc_ref[pl.ds(pl.multiple_of((1 - mine) * half, half), half), :].astype(BF)


def attention_grads(rows, grads, stack, o, place):
    local, width = o.shape[-1], rows[0].shape[-1]
    return kernel_call(
        attention_grads_kernel,
        "attention_grads",
        [shape((2 * local, width), BF)] * 2,
        3_000_000_000,
        *rows,
        *grads,
        stack,
        o,
        scalar(place),
        scratch=[pltpu.VMEM((4 * local, width), F32)],
    )


def gelu_parts(u):
    square = u * u
    t = jnp.tanh(GELU_SCALE * (u + GELU_CUBE * (square * u)))
    plus = 0.5 * (1.0 + t)
    slope = plus + 0.5 * u * (1.0 - t * t) * (GELU_SCALE * (1.0 + (3.0 * GELU_CUBE) * square))
    return u * plus, slope


def up_rows(layer, rows, up_ref, bias_ref):
    u = mxu(rows, up_ref[layer], NN) + of_layer(bias_ref, layer)
    z, slope = gelu_parts(u)
    return z.astype(BF), slope


def forward_kernel(layer, c0, c1, c2, c3, up_ref, bias_ref, down_ref, p0, p1, p2, p3, z_ref, slope_ref):
    size = 256
    for block, (rows_ref, out_ref) in enumerate(zip((c0, c1, c2, c3), (p0, p1, p2, p3))):

        def step(i, carry):
            at = pl.ds(pl.multiple_of(i * size, size), size)
            z, slope = up_rows(layer, rows_ref[at, :], up_ref, bias_ref)
            z_ref[block, at, :] = z
            slope_ref[block, at, :] = slope.astype(BF)
            out_ref[at, :] = mxu(z, down_ref[layer], NN).astype(BF)
            return carry

        lax.fori_loop(0, rows_ref.shape[0] // size, step, 0)


def feed_forward(layer, blocks, w_up, up_bias, w_down):
    units = w_up.shape[2]
    size = blocks[0].shape[0]
    outs = [shape(blocks[0].shape, BF)] * 4 + [shape((4, size, units), BF)] * 2
    made = kernel_call(functools.partial(forward_kernel, layer), "feed_forward", outs, 4_000_000_000, *blocks, w_up, up_bias, w_down)
    return made[:4], made[4:]


def down_kernel(layer, z_ref, down_ref, p0, p1, p2, p3):
    size = 256
    for block, out_ref in enumerate((p0, p1, p2, p3)):

        def step(i, carry):
            at = pl.ds(pl.multiple_of(i * size, size), size)
            out_ref[at, :] = mxu(z_ref[block, at, :], down_ref[layer], NN).astype(BF)
            return carry

        lax.fori_loop(0, out_ref.shape[0] // size, step, 0)


def down_product(layer, z, w_down):
    outs = [shape((z.shape[1], w_down.shape[2]), BF)] * 4
    return kernel_call(functools.partial(down_kernel, layer), "down_product", outs, 1_500_000_000, z, w_down)


def back_kernel(layer, g0, g1, g2, g3, slope_ref, up_ref, down_ref, p0, p1, p2, p3, gu_ref, sums_ref):
    size = 256
    sums_ref[...] = jnp.zeros(sums_ref.shape, F32)
    for block, (grad_ref, out_ref) in enumerate(zip((g0, g1, g2, g3), (p0, p1, p2, p3))):

        def step(i, carry):
            at = pl.ds(pl.multiple_of(i * size, size), size)
            gz = mxu(grad_ref[at, :], down_ref[layer], NT)
            gu = (gz * slope_ref[block, at, :].astype(F32)).astype(BF)
            gu_ref[block, at, :] = gu
            sums_ref[...] += fold_rows(gu.astype(F32))
            out_ref[at, :] = mxu(gu, up_ref[layer], NT).astype(BF)
            return carry

        lax.fori_loop(0, grad_ref.shape[0] // size, step, 0)


def feed_back(layer, blocks, slope, w_up, w_down):
    size, units = blocks[0].shape[0], w_up.shape[2]
    outs = [shape(blocks[0].shape, BF)] * 4 + [shape((4, size, units), BF), shape((8, units), F32)]
    made = kernel_call(functools.partial(back_kernel, layer), "feed_back", outs, 4_000_000_000, *blocks, slope, w_up, w_down)
    return made[:4], made[4:]


def feed_grads_into(rows_refs, grad_refs, z_ref, gu_ref, place_ref, out_refs, both_ref):
    unused, units, width = both_ref.shape
    step = 256
    for start in range(0, units, step):
        rows = slice(start, start + step)
        down = sum(mxu(z_ref[i, :, rows], g[...], TN) for i, g in enumerate(grad_refs))
        both_ref[0, rows, :] = down.astype(BF)
        up = sum(mxu(c[:, rows], gu_ref[i], TN) for i, c in enumerate(rows_refs))
        both_ref[1, rows, :] = up.astype(BF)
    mine = place_ref[0] & 1
    parts = len(out_refs) // 2
    size = units // parts
    for part in range(parts):
        rows = slice(part * size, (part + 1) * size)
        out_refs[2 * part][...] = both_ref[mine, rows, :]
        out_refs[2 * part + 1][...] = both_ref[1 - mine, rows, :]


def feed_grads_kernel(*refs):
    feed_grads_into(refs[:4], refs[4:8], refs[8], refs[9], refs[10], refs[11:-1], refs[-1])


def feed_grads(rows, grads, z, gu, place, parts):
    units, width = z.shape[-1], rows[0].shape[-1]
    made = kernel_call(
        feed_grads_kernel,
        "feed_grads",
        [shape((units // parts, width), BF)] * (2 * parts),
        4_000_000_000,
        *rows,
        *grads,
        z,
        gu,
        scalar(place),
        scratch=[pltpu.VMEM((2, units, width), BF)],
    )
    return [made[2 * i : 2 * i + 2] for i in range(parts)]


def both_kernel(layer, *refs):
    rows_refs, grad_refs, (up_ref, bias_ref, down_ref, place_ref) = refs[:4], refs[4:8], refs[8:12]
    out_refs, (z_ref, sums_ref, keep_ref, send_ref, gu_ref, both_ref) = refs[12:16], refs[16:]
    sums_ref[...] = jnp.zeros(sums_ref.shape, F32)
    for block in range(4):
        gz = mxu(grad_refs[block][...], down_ref[layer], NT)
        z, slope = up_rows(layer, rows_refs[block][...], up_ref, bias_ref)
        z_ref[block] = z
        gu = (gz * slope).astype(BF)
        gu_ref[block] = gu
        sums_ref[...] += fold_rows(gu.astype(F32))
        out_refs[block][...] = mxu(gu, up_ref[layer], NT).astype(BF)
    feed_grads_into(rows_refs, grad_refs, z_ref, gu_ref, place_ref, (keep_ref, send_ref), both_ref)


def feed_both(layer, blocks, grads, w_up, up_bias, w_down, place):
    size, units = blocks[0].shape[0], w_up.shape[2]
    width = blocks[0].shape[1]
    outs = [shape(blocks[0].shape, BF)] * 4 + [shape((4, size, units), BF), shape((8, units), F32)]
    outs += [shape((units, width), BF)] * 2
    made = kernel_call(
        functools.partial(both_kernel, layer),
        "feed_both",
        outs,
        10_000_000_000,
        *blocks,
        *grads,
        w_up,
        up_bias,
        w_down,
        scalar(place),
        scratch=[pltpu.VMEM((4, size, units), BF), pltpu.VMEM((2, units, width), BF)],
    )
    return made[:4], made[4:6], made[6:]


def partners(bits, bit):
    return [(i, i ^ (1 << bit)) for i in range(1 << len(bits))]


def crossed(place, swapped):
    other = (place & ~3) | ((place & 1) << 1) | ((place >> 1) & 1)
    return jnp.where(swapped == 1, other, place)


def crossed_partners(bits, bit, crossing):
    pairs = []
    for i in range(1 << len(bits)):
        for t in range(4):
            taken = bit ^ 1 if crossing and bit < 2 and t & 1 else bit
            pairs.append((i * 4 + t, (i ^ (1 << taken)) * 4 + t))
    return pairs


def halve_kernel(bit, keep_ref, got_ref, place_ref, out_keep_ref, out_send_ref):
    half = out_keep_ref.shape[0]
    mine = (place_ref[0] >> bit) & 1
    for out_ref, which in ((out_send_ref, 1 - mine), (out_keep_ref, mine)):
        at = pl.ds(pl.multiple_of(which * half, half), half)
        out_ref[...] = (keep_ref[at, :].astype(F32) + got_ref[at, :].astype(F32)).astype(BF)


def halve(keep, got, bit, place):
    rows, width = keep.shape
    outs = [shape((rows // 2, width), BF)] * 2
    return kernel_call(
        functools.partial(halve_kernel, bit), "halve", outs, 200_000_000, keep, got, scalar(place)
    )


def join_kernel(bit, own_ref, got_ref, place_ref, out_ref):
    half = own_ref.shape[0]
    mine = (place_ref[0] >> bit) & 1
    out_ref[pl.ds(pl.multiple_of(mine * half, half), half), :] = own_ref[...]
    out_ref[pl.ds(pl.multiple_of((1 - mine) * half, half), half), :] = got_ref[...]


def join(own, got, bit, place):
    rows, width = own.shape
    return kernel_call(
        functools.partial(join_kernel, bit),
        "join",
        [shape((2 * rows, width), BF)],
        200_000_000,
        own,
        got,
        scalar(place),
    )[0]


class PageSum:
    def __init__(self, halves, bits, places, crossing):
        self.own, send = halves
        self.bits, self.place, self.crossing = bits, places[crossing], crossing
        self.plan = [self.cut, self.add, self.turn, self.back]
        self.got = self.swap(send, 0)

    def swap(self, values, bit):
        self.sent = values
        return lax.ppermute(values, ("dp", "tensor"), crossed_partners(self.bits, bit, self.crossing))

    def cut(self, got):
        self.own, send = halve(self.own, got, 1, self.place)
        return self.swap(send, 1)

    def add(self, got):
        self.own = self.own + got
        return self.swap(self.own, 2)

    def turn(self, got):
        self.own = self.own + got
        for bit in self.bits[3:]:
            self.own = self.own + self.swap(self.own, bit)
        return self.swap(self.own, 1)

    def back(self, got):
        self.own = join(self.own, got, 1, self.place)
        return self.swap(self.own, 0)

    def step(self, token):
        self.got = self.plan.pop(0)(tied(self.got, token))
        return self.sent

    def ended(self):
        return self.own, self.got


def sum_small(values, axis, bits, count):
    for bit in bits:
        values = values + lax.ppermute(values, axis, partners(range(count), bit))
    return values


def row_sum(values):
    return jnp.sum(values, axis=0, keepdims=True)


def pack_rows_kernel(ones0, twos0, ones1, twos1, last_ref, out_ref):
    out_ref[...] = jnp.zeros(out_ref.shape, F32)
    for layer, (one_ref, two_ref) in enumerate(((ones0, twos0), (ones1, twos1))):
        down = ones1[2] if layer == 0 else last_ref[...]
        members = [one_ref[0], one_ref[1], two_ref[2], two_ref[0], two_ref[1], down]
        for i, member in enumerate(members):
            out_ref[2 * i + layer : 2 * i + layer + 1, :] = row_sum(member)
    out_ref[12:13, :] = row_sum(ones0[2])


def pack_rows(ones, twos, last):
    return kernel_call(
        pack_rows_kernel,
        "pack_rows",
        [shape((16, last.shape[-1]), F32)],
        1_000_000,
        ones[0],
        twos[0],
        ones[1],
        twos[1],
        last,
    )[0]


def pack_all_kernel(rows_ref, qv0, qv1, up0, up1, rel0, rel1, out_ref):
    local = qv0.shape[-1]
    out_ref[:16, :] = rows_ref[...]
    out_ref[16:, :] = jnp.zeros((32, out_ref.shape[1]), F32)
    for layer, (qv_ref, up_ref, rel_ref) in enumerate(((qv0, up0, rel0), (qv1, up1, rel1))):
        out_ref[16 + layer : 17 + layer, :] = row_sum(up_ref[...])
        for i in range(2):
            out_ref[18 + 2 * layer + i : 19 + 2 * layer + i, :local] = row_sum(qv_ref[i])
        heads = rel_ref.shape[0] // 24
        for h in range(heads):
            start = (layer * heads + h) * 128
            out_ref[24:48, start : start + 32] = rel_ref[h * 24 : h * 24 + 24, :]


def pack_all(rows, qv_sums, up_sums, rel_sums):
    return kernel_call(
        pack_all_kernel,
        "pack_all",
        [shape((48, rows.shape[-1]), F32)],
        1_000_000,
        rows,
        *qv_sums,
        *up_sums,
        *rel_sums,
    )[0]


def unpack_kernel(all_ref, *out_refs):
    rows, mask_ref, up_ref, qv_ref, rel_ref = out_refs[:6], *out_refs[6:]
    for i, row_ref in enumerate(rows):
        row_ref[...] = all_ref[2 * i : 2 * i + 2, :]
    mask_ref[...] = all_ref[12:13, :]
    up_ref[...] = all_ref[16:18, :]
    heads, layers, entries = rel_ref.shape
    local = qv_ref.shape[-1]
    for layer in range(layers):
        qv_ref[layer] = all_ref[18 + 2 * layer : 20 + 2 * layer, :local]
        for h in range(heads):
            start = (layer * heads + h) * 128
            for j in range(6):
                lines = [all_ref[24 + 4 * j + r : 25 + 4 * j + r, start : start + 32] for r in range(4)]
                size = min(128, entries - 128 * j)
                line = jnp.concatenate(lines, axis=1)[:, :size]
                rel_ref[h, layer : layer + 1, 128 * j : 128 * j + size] = line


def unpack(values, heads, entries):
    width = values.shape[-1]
    outs = [shape((LAYERS, width), F32)] * 6 + [shape((1, width), F32), shape((LAYERS, width), F32)]
    outs += [shape((LAYERS, 2, heads * HEAD_DIM), F32), shape((heads, LAYERS, entries), F32)]
    return kernel_call(unpack_kernel, "unpack", outs, 1_000_000, values)


def assemble_kernel(layer, pieces, own_ref, got_ref, place_ref, *refs):
    out_refs, (stage_ref, sems) = refs[-2 - len(pieces) : -2], refs[-2:]
    half = own_ref.shape[0]
    mine = place_ref[0] & 1
    stage_ref[pl.ds(pl.multiple_of(mine * half, half), half), :] = own_ref[...].astype(F32)
    stage_ref[pl.ds(pl.multiple_of((1 - mine) * half, half), half), :] = got_ref[...].astype(F32)
    copies = []
    for out_ref, parts in zip(out_refs, pieces):
        for index, start, rows in parts:
            target = out_ref.at[(layer,) + index]
            source = stage_ref.at[pl.ds(start, rows), :]
            copies.append(pltpu.make_async_copy(source, target, sems.at[len(copies)]))
    for copy in copies:
        copy.start()
    for copy in copies:
        copy.wait()


def assemble(layer, name, pieces, outs, own, got, place, before):
    rows, width = own.shape
    anywhere = pl.BlockSpec(memory_space=pl.ANY)
    count = sum(len(parts) for parts in pieces)
    return pl.pallas_call(
        functools.partial(assemble_kernel, layer, pieces),
        out_shape=tuple(outs),
        in_specs=[VMEM, VMEM, pl.BlockSpec(memory_space=pltpu.SMEM)] + [anywhere] * len(before),
        out_specs=tuple([anywhere] * len(outs)),
        scratch_shapes=[pltpu.VMEM((2 * rows, width), F32), pltpu.SemaphoreType.DMA((count,))],
        input_output_aliases={3 + i: i for i in range(len(before))},
        name=name,
        compiler_params=pltpu.CompilerParams(vmem_limit_bytes=VMEM_GRANT),
        cost_estimate=pl.CostEstimate(flops=1_000_000, bytes_accessed=rows * width, transcendentals=0),
    )(own, got, place, *before)


def assemble_feed(layer, part, parts, sums, place, before=()):
    own, got = sums.ended()
    size, width = own.shape
    pieces = [[((pl.ds(part * size, size),), 0, size)], [((pl.ds(part * size, size),), size, size)]]
    outs = [shape((LAYERS, parts * size, width), F32)] * 2
    return assemble(layer, "assemble_feed", pieces, outs, own, got, place, before)


def assemble_attention(layer, sums, place, before=()):
    own, got = sums.ended()
    local, width = own.shape[0] // 2, own.shape[1]
    pieces = [[((), 0, local)], [((t,), (t + 1) * local, local) for t in range(3)]]
    outs = [shape((LAYERS, local, width), F32), shape((LAYERS, 3, local, width), F32)]
    return assemble(layer, "assemble_attention", pieces, outs, own, got, place, before)


def shards(
    n_dp,
    patch_rows,
    cotangent,
    mask_flags,
    pad_flags,
    buckets,
    mask_emb,
    ln1_gain,
    ln1_bias,
    w_qkv,
    qv_bias,
    rel_table,
    w_out,
    out_bias,
    ln2_gain,
    ln2_bias,
    w_up,
    up_bias,
    w_down,
    down_bias,
):
    member = lax.axis_index("tensor").reshape(1).astype(jnp.int32)
    straight = lax.axis_index("dp").reshape(1).astype(jnp.int32)
    places = [straight, crossed(straight, lax.axis_index("tensor") & 1)]
    bits = list(range(n_dp.bit_length() - 1))
    pages = patch_rows.shape[1]
    heads, entries = rel_table.shape[1:]
    last = LAYERS - 1
    masked = mask_flags.T
    w_qkv = jnp.swapaxes(w_qkv, 2, 3)

    hidden, own, last_own, last_sum = first_norm(
        patch_rows, cotangent, masked, mask_emb.reshape(1, -1), ln1_gain, ln1_bias
    )
    rel_bias, ordered, pad_bias = bias_of_buckets(jnp.swapaxes(rel_table, 0, 1), buckets, pad_flags.T, member)
    blocks = spread(own, (rel_bias,))
    last_blocks = spread(tied(last_own, blocks[3]))

    kept = []
    for layer in range(LAYERS):
        rows_one, before = blocks, hidden
        partial, saved = attention(layer, rows_one, w_qkv, qv_bias, rel_bias, pad_bias, w_out)
        near, far, unused = collect(partial)
        middle, own = add_norm(hidden, near + [far], (layer, layer), out_bias, ln2_gain, ln2_bias)
        rows_two = spread(own)
        if layer == last:
            partial, (z, up_sums), mlp = feed_both(
                layer, rows_two, last_blocks, w_up, up_bias, w_down, places[1]
            )
            kept.append((rows_one, before, saved, middle, rows_two, z, None))
        else:
            partial, (z, slope) = feed_forward(layer, rows_two, w_up, up_bias, w_down)
            kept.append((rows_one, before, saved, middle, rows_two, z, slope))
            near, far, unused = collect(partial)
            hidden, own = add_norm(middle, near + [far], (layer, layer + 1), down_bias, ln1_gain, ln1_bias)
            blocks = spread(own)

    rows_one, before, saved, middle, rows_two, z, unused = kept[last]
    near, far, sent = collect(partial)
    mlp1 = PageSum(mlp, bits, places, 1)
    g1, low, twos1 = norm_back(last_own, near + [far], middle, last, ln2_gain)
    result_parts = down_product(last, tied(z, low), w_down)
    token = mlp1.step(result_parts[0])
    out_blocks = spread(low, (result_parts, token))
    partial, (stack, totals, qv1) = attention_back(last, out_blocks, saved, w_qkv, w_out)
    near, far, sent = collect(partial)
    mix = attention_grads(rows_one, out_blocks, tied(stack, sent), saved[-1], places[1])
    mix1 = PageSum(mix, bits, places, 1)
    token = mlp1.step(mix)
    far = tied(far, token)
    grad, low, ones1 = norm_back(g1, near + [far], before, last, ln1_gain)
    rel1 = sum_by_bucket(tied(totals, low), ordered)
    token = mix1.step(rel1)
    grad_blocks = spread(low, (token,))
    up1 = up_sums

    rows_one, before, saved, middle, rows_two, z, slope = kept[0]
    partial, (gu, up0) = feed_back(0, grad_blocks, slope, w_up, w_down)
    near, far, sent = collect(partial)
    mlp = feed_grads(rows_two, grad_blocks, tied(z, sent), gu, places[1], 2)
    mlp0a, mlp0b = [PageSum(x, bits, places, 1) for x in mlp]
    token = mix1.step(mlp)
    far = tied(far, token)
    g1, low, twos0 = norm_back(grad, near + [far], middle, 0, ln2_gain)
    token = mlp1.step(low)
    token = mlp0a.step(token)
    out_blocks = spread(low, (token,))
    partial, (stack, totals, qv0) = attention_back(0, out_blocks, saved, w_qkv, w_out)
    near, far, sent = collect(partial)
    mix = attention_grads(rows_one, out_blocks, tied(stack, sent), saved[-1], places[1])
    mix0 = PageSum(mix, bits, places, 1)
    token = mlp1.step(mix)
    token = mlp0b.step(token)
    token = mix1.step(token)
    far = tied(far, token)
    grad, ones0 = last_norm_back(g1, near + [far], before, ln1_gain, masked)

    def hop(values, axis, order, bit):
        return lax.ppermute(values, axis, partners(order, bit))

    rows = pack_rows((ones0, ones1), (twos0, twos1), last_sum)
    rows_got = hop(rows, "tensor", [0, 1], 0)
    token = rows
    token = mlp0a.step(token)
    token = mix0.step(token)
    rows = token = rows + tied(rows_got, token)
    rows_got = hop(rows, "tensor", [0, 1], 1)
    rel0 = token = sum_by_bucket(tied(totals, token), ordered)
    result_near, result_far, unused = collect([tied(p, rel0) for p in result_parts])
    token = mlp0b.step(token)
    small = pack_all(rows + tied(rows_got, token), (qv0, qv1), (up0, up1), (rel0, rel1))
    small_got = hop(small, "dp", bits, 0)
    token = small
    token = mlp0a.step(token)
    token = mix0.step(token)
    small = token = small + tied(small_got, token)
    small_got = hop(small, "dp", bits, 1)
    result = token = last_result(
        kept[last][3], result_near + [tied(result_far, token)], last, down_bias, pages
    )
    token = mix1.step(token)
    token = mlp0b.step(token)
    small = token = small + tied(small_got, token)
    small_got = hop(small, "dp", bits, 2)
    token = mlp0a.step(token)
    d_mlp = assemble_feed(last, 0, 1, mlp1, tied(places[1], token))
    token = d_mlp[0]
    token = mix0.step(token)
    small = small + tied(small_got, token)
    small = token = sum_small(small, "dp", bits[3:], len(bits))
    token = mlp0b.step(token)
    d_mix = assemble_attention(last, mix1, tied(places[1], token))
    token = d_mix[0]
    token = mix0.step(token)
    d_mlp = assemble_feed(0, 0, 2, mlp0a, tied(places[1], token), d_mlp)
    token = d_mlp[0]
    d_mlp = assemble_feed(0, 1, 2, mlp0b, tied(places[1], token), d_mlp)
    token = d_mlp[0]
    d_mix = assemble_attention(0, mix0, tied(places[1], token), d_mix)
    token = d_mix[0]
    small = unpack(small, heads, entries)
    d_ln1_gain, d_ln1_bias, d_out_bias, d_ln2_gain, d_ln2_bias, d_down_bias, d_mask, d_up_bias, d_qv, d_rel = small
    return (
        result,
        grad,
        d_mask.reshape(-1),
        d_ln1_gain,
        d_ln1_bias,
        jnp.swapaxes(d_mix[1], 2, 3),
        d_qv,
        jnp.swapaxes(d_rel, 0, 1),
        d_mix[0],
        d_out_bias,
        d_ln2_gain,
        d_ln2_bias,
        d_mlp[1],
        d_up_bias,
        d_mlp[0],
        d_down_bias,
    )


def solution(mesh):
    rows = P("tensor", "dp", None)
    units = P(None, "tensor", None)
    columns = P(None, None, "tensor")
    whole = P()
    return jax.shard_map(
        functools.partial(shards, mesh.shape["dp"]),
        mesh=mesh,
        in_specs=(
            rows,
            rows,
            P("tensor", "dp"),
            P(None, "dp"),
            whole,
            whole,
            whole,
            whole,
            P(None, None, None, "tensor"),
            columns,
            units,
            units,
            whole,
            whole,
            whole,
            columns,
            P(None, "tensor"),
            units,
            whole,
        ),
        out_specs=(
            rows,
            rows,
            whole,
            whole,
            whole,
            P(None, None, None, "tensor"),
            columns,
            units,
            units,
            whole,
            whole,
            whole,
            columns,
            P(None, "tensor"),
            units,
            whole,
        ),
        check_vma=False,
    )
```

```python
import functools

import jax
import jax.numpy as jnp
from jax import lax
from jax.experimental import pallas as pl
from jax.experimental.pallas import tpu as pltpu
from jax.sharding import PartitionSpec as P

HEAD_DIM = 64
BUCKETS = 732
LAYERS = 2
EPSILON = 1e-06
VMEM_GRANT = 10 * 1024 * 1024
GELU_SCALE = 0.7978845608028654
GELU_CUBE = 0.044715

BF = jnp.bfloat16
F32 = jnp.float32
CORE = [(i, i ^ 1) for i in range(4)]
CHIP = [(i, i ^ 2) for i in range(4)]
VMEM = pl.BlockSpec(memory_space=pltpu.VMEM)
NN = (((1,), (0,)), ((), ()))
NT = (((1,), (1,)), ((), ()))
TN = (((0,), (0,)), ((), ()))


def shape(dims, kind):
    return jax.ShapeDtypeStruct(dims, kind)


def scalar(values):
    return (values, pl.BlockSpec(memory_space=pltpu.SMEM))


def kernel_call(body, name, outs, flops, *operands, scratch=()):
    specs = [x[1] if isinstance(x, tuple) else VMEM for x in operands]
    operands = [x[0] if isinstance(x, tuple) else x for x in operands]
    moved = sum(x.size * x.dtype.itemsize for x in operands) + sum(
        o.size * o.dtype.itemsize for o in outs
    )
    return pl.pallas_call(
        body,
        out_shape=tuple(outs),
        in_specs=specs,
        out_specs=tuple([VMEM] * len(outs)),
        scratch_shapes=list(scratch),
        name=name,
        compiler_params=pltpu.CompilerParams(vmem_limit_bytes=VMEM_GRANT),
        cost_estimate=pl.CostEstimate(flops=flops // 100, bytes_accessed=moved // 100, transcendentals=0),
    )(*operands)


def mxu(left, right, dims):
    return lax.dot_general(left, right, dims, preferred_element_type=F32)


def swap_core(values):
    return lax.ppermute(values, "tensor", CORE)


def swap_chip(values):
    return lax.ppermute(values, "tensor", CHIP)


def tied(values, token):
    return lax.optimization_barrier((values, token))[0]


def spread(own, meanwhile=()):
    far = swap_chip(own)
    near = swap_core(own)
    if meanwhile:
        far = tied(far, meanwhile)
    return [own, near, far, swap_core(far)]


def collect(partial):
    pair_far = partial[2] + swap_core(partial[3])
    return [partial[0], swap_core(partial[1])], swap_chip(pair_far), pair_far


def bias_kernel(table_ref, index_ref, pad_ref, member_ref, out_ref, ordered_ref, bias_ref):
    heads, layers, entries = table_ref.shape
    lanes = 128
    chunks = (entries + lanes - 1) // lanes
    member = member_ref[0]
    low, high = member & 1, member >> 1
    block = index_ref.shape[0] // 4

    def picked(ref, rows, half):
        tile = ref[rows, pl.ds(pl.multiple_of((half ^ high) * lanes, lanes), lanes)]
        return jnp.where(low == 1, jnp.concatenate([tile[:, block:], tile[:, :block]], axis=1), tile)

    for half in range(2):
        columns = slice(half * lanes, half * lanes + lanes)
        pads = picked(pad_ref, slice(None), half)
        bias_ref[:, 0, columns] = jnp.where(pads == 1, -1000000000.0, 0.0)

    def line_of(layer, head, chunk):
        size = min(lanes, entries - chunk * lanes)
        line = table_ref[head, layer : layer + 1, chunk * lanes : chunk * lanes + size].astype(F32)
        return jnp.concatenate([line, jnp.zeros((1, lanes - size), F32)], axis=1) if size < lanes else line

    lines = [[line_of(l, h, c) for c in range(chunks)] for l in range(layers) for h in range(heads)]

    def rows_step(step, carry):
        start = (member ^ (step // 4)) * block + (step % 4) * 16
        rows = pl.ds(pl.multiple_of(start, 16), 16)
        place = pl.ds(pl.multiple_of(step * 16, 16), 16)
        for half in range(2):
            columns = slice(half * lanes, half * lanes + lanes)
            index = picked(index_ref, rows, half)
            ordered_ref[place, columns] = index
            lane, chunk = index & (lanes - 1), index // lanes
            here = [chunk == c for c in range(chunks)]
            for table in range(layers * heads):
                total = jnp.zeros((16, lanes), F32)
                for c in range(chunks):
                    line = jnp.broadcast_to(lines[table][c], (16, lanes))
                    total = jnp.where(here[c], jnp.take_along_axis(line, lane, axis=1), total)
                out_ref[table // heads, table % heads, place, columns] = total.astype(out_ref.dtype)
        return carry

    lax.fori_loop(0, index_ref.shape[0] // 16, rows_step, 0)


def bias_of_buckets(tables, buckets, pads, member):
    heads, layers, entries = tables.shape
    pages, length = pads.shape
    outs = [shape((layers, heads) + buckets.shape, BF), shape(buckets.shape, jnp.int32)]
    outs += [shape((pages, 1, length), F32)]
    return kernel_call(
        bias_kernel, "bias_of_buckets", outs, 4_000_000_000, tables, buckets, pads, scalar(member)
    )


def bucket_kernel(values_ref, index_ref, out_ref):
    heads, size, width = values_ref.shape
    chunk = 32

    def step(i, total):
        start = pl.multiple_of(i * chunk, chunk)
        index = index_ref[pl.ds(start, chunk), :]
        left, right = [], []
        for r in range(chunk):
            row = index[r : r + 1, :]
            at_high = lax.broadcasted_iota(jnp.int32, (24, width), 0) == (row >> 5)
            at_low = lax.broadcasted_iota(jnp.int32, (32, width), 0) == (row & 31)
            right.append(jnp.where(at_low, 1.0, 0.0).astype(BF))
            left.append(
                jnp.concatenate(
                    [
                        jnp.where(at_high, values_ref[h, pl.ds(start + r, 1), :], 0.0).astype(BF)
                        for h in range(heads)
                    ],
                    0,
                )
            )
        return total + mxu(jnp.concatenate(left, 1), jnp.concatenate(right, 1), NT)

    out_ref[...] = lax.fori_loop(0, size // chunk, step, jnp.zeros((heads * 24, 32), F32))


def sum_by_bucket(values, buckets):
    heads = values.shape[0]
    return kernel_call(
        bucket_kernel, "sum_by_bucket", [shape((heads * 24, 32), F32)], 6_000_000_000, values, buckets
    )[0]


def normal_of(values):
    center = values - jnp.mean(values, axis=-1, keepdims=True)
    inverse = lax.rsqrt(jnp.mean(center * center, axis=-1, keepdims=True) + EPSILON)
    return center * inverse, inverse


def of_layer(ref, layer):
    return ref[layer : layer + 1, :].astype(F32)


def mask_columns(masked_ref):
    pages, size = masked_ref.shape
    row = lax.broadcasted_iota(jnp.int32, (size, size), 0)
    diagonal = row == lax.broadcasted_iota(jnp.int32, (size, size), 1)
    flags = masked_ref[...].astype(F32)
    spreads = [jnp.where(diagonal, flags[page : page + 1, :], 0.0) for page in range(pages)]
    return [jnp.sum(values, axis=1, keepdims=True) == 1.0 for values in spreads]


def first_norm_kernel(
    rows_ref, grads_ref, masked_ref, embed_ref, gain_ref, shift_ref, hidden_ref, normed_ref, grad_ref, sums_ref
):
    size, pages, width = rows_ref.shape
    gain, shift = of_layer(gain_ref, 0), of_layer(shift_ref, 0)
    total = jnp.zeros((8, width), F32)
    masks = mask_columns(masked_ref)
    for page in range(pages):
        at = slice(page * size, page * size + size)
        masked = masks[page]
        rows = jnp.where(masked, embed_ref[...].astype(F32), rows_ref[:, page, :].astype(F32))
        hidden_ref[at, :] = rows
        normed_ref[at, :] = (normal_of(rows)[0] * gain + shift).astype(BF)
        grad = grads_ref[:, page, :]
        grad_ref[at, :] = grad
        total = total + fold_rows(grad.astype(F32))
    sums_ref[...] = total


def first_norm(rows, grads, masked, embed, gains, shifts):
    size, pages, width = rows.shape
    flat = (size * pages, width)
    return kernel_call(
        first_norm_kernel,
        "first_norm",
        [shape(flat, F32), shape(flat, BF), shape(flat, BF), shape((8, width), F32)],
        1_000_000_000,
        rows,
        grads,
        masked,
        embed,
        gains,
        shifts,
    )


def norm_kernel(layers, hidden_ref, one_ref, two_ref, three_ref, bias_ref, gain_ref, shift_ref, out_ref, normed_ref):
    size = 64
    bias = of_layer(bias_ref, layers[0])
    gain, shift = of_layer(gain_ref, layers[1]), of_layer(shift_ref, layers[1])

    def step(i, carry):
        at = pl.ds(pl.multiple_of(i * size, size), size)
        total = one_ref[at, :].astype(F32) + two_ref[at, :].astype(F32) + three_ref[at, :].astype(F32)
        rows = hidden_ref[at, :] + total + bias
        out_ref[at, :] = rows
        normed_ref[at, :] = (normal_of(rows)[0] * gain + shift).astype(BF)
        return carry

    lax.fori_loop(0, hidden_ref.shape[0] // size, step, 0, unroll=True)


def add_norm(hidden, terms, layers, biases, gains, shifts):
    return kernel_call(
        functools.partial(norm_kernel, layers),
        "add_norm",
        [shape(hidden.shape, F32), shape(hidden.shape, BF)],
        1_000_000_000,
        hidden,
        *terms,
        biases,
        gains,
        shifts,
    )


def result_kernel(layer, hidden_ref, one_ref, two_ref, three_ref, bias_ref, out_ref):
    size, pages, unused = out_ref.shape
    bias = of_layer(bias_ref, layer)
    for page in range(pages):
        at = slice(page * size, page * size + size)
        total = one_ref[at, :].astype(F32) + two_ref[at, :].astype(F32) + three_ref[at, :].astype(F32)
        out_ref[:, page, :] = (hidden_ref[at, :] + total + bias).astype(BF)


def last_result(hidden, terms, layer, biases, pages):
    rows, width = hidden.shape
    return kernel_call(
        functools.partial(result_kernel, layer),
        "last_result",
        [shape((rows // pages, pages, width), BF)],
        1_000_000_000,
        hidden,
        *terms,
        biases,
    )[0]


def fold_rows(values):
    return jnp.sum(values.reshape(-1, 8, values.shape[-1]), axis=0)


def norm_back_step(at, grad_ref, terms, values_ref, gain, sums_ref):
    total = sum(term[at, :].astype(F32) for term in terms)
    normal, inverse = normal_of(values_ref[at, :])
    scaled = total * gain
    inner = scaled - jnp.mean(scaled, -1, keepdims=True)
    inner = inner - normal * jnp.mean(scaled * normal, -1, keepdims=True)
    grad = grad_ref[at, :].astype(F32) + inner * inverse
    sums_ref[0] += fold_rows(total * normal)
    sums_ref[1] += fold_rows(total)
    return grad


def norm_back_kernel(layer, grad_ref, one_ref, two_ref, three_ref, values_ref, gain_ref, out_ref, low_ref, sums_ref):
    size = 64
    sums_ref[...] = jnp.zeros(sums_ref.shape, F32)

    def step(i, carry):
        at = pl.ds(pl.multiple_of(i * size, size), size)
        terms = (one_ref, two_ref, three_ref)
        grad = norm_back_step(at, grad_ref, terms, values_ref, of_layer(gain_ref, layer), sums_ref)
        sums_ref[2] += fold_rows(grad)
        out_ref[at, :] = grad
        low_ref[at, :] = grad.astype(BF)
        return carry

    lax.fori_loop(0, grad_ref.shape[0] // size, step, 0, unroll=True)


def norm_back(grad, terms, values, layer, gains):
    return kernel_call(
        functools.partial(norm_back_kernel, layer),
        "norm_back",
        [shape(grad.shape, F32), shape(grad.shape, BF), shape((3, 8, grad.shape[-1]), F32)],
        1_500_000_000,
        grad,
        *terms,
        values,
        gains,
    )


def last_norm_back_kernel(
    grad_ref, one_ref, two_ref, three_ref, values_ref, gain_ref, masked_ref, out_ref, sums_ref
):
    size, pages, unused = out_ref.shape
    sums_ref[...] = jnp.zeros(sums_ref.shape, F32)
    masks = mask_columns(masked_ref)
    for page in range(pages):
        at = slice(page * size, page * size + size)
        terms = (one_ref, two_ref, three_ref)
        grad = norm_back_step(at, grad_ref, terms, values_ref, of_layer(gain_ref, 0), sums_ref)
        masked = masks[page]
        sums_ref[2] += fold_rows(jnp.where(masked, grad, 0.0))
        out_ref[:, page, :] = jnp.where(masked, 0.0, grad)


def last_norm_back(grad, terms, values, gains, masked):
    pages, size = masked.shape
    width = grad.shape[-1]
    return kernel_call(
        last_norm_back_kernel,
        "last_norm_back",
        [shape((size, pages, width), F32), shape((3, 8, width), F32)],
        1_500_000_000,
        grad,
        *terms,
        values,
        gains,
        masked,
    )


def page_rows(refs, page, size):
    at = pl.ds(pl.multiple_of(page * size, size), size)
    return jnp.concatenate([ref[at, :] for ref in refs], axis=0)


def put_page(refs, page, size, values):
    at = pl.ds(pl.multiple_of(page * size, size), size)
    for i, ref in enumerate(refs):
        ref[at, :] = values[i * size : (i + 1) * size]


def head_masks(heads, kind):
    lane = lax.broadcasted_iota(jnp.int32, (1, heads * HEAD_DIM), 1)
    return [jnp.where((lane // HEAD_DIM) == h, 1.0, 0.0).astype(kind) for h in range(heads)]


def project_rows(layer, rows, w_ref, bias_ref):
    q = ((mxu(rows, w_ref[layer, 0], NT) + bias_ref[layer, 0:1, :].astype(F32)) * HEAD_DIM**-0.5).astype(BF)
    k = mxu(rows, w_ref[layer, 1], NT).astype(BF)
    v = (mxu(rows, w_ref[layer, 2], NT) + bias_ref[layer, 1:2, :].astype(F32)).astype(BF)
    return q, k, v


def project_pair(layer, x0, x1, w_ref, bias_ref, outs):
    size = x0.shape[0]
    rows = jnp.concatenate([x0[...], x1[...]], axis=0)
    for out_ref, made in zip(outs, project_rows(layer, rows, w_ref, bias_ref)):
        out_ref[0], out_ref[1] = made[:size], made[size:]


def project_kernel(layer, x0, x1, w_ref, bias_ref, q_ref, k_ref, v_ref):
    project_pair(layer, x0, x1, w_ref, bias_ref, (q_ref, k_ref, v_ref))


def project(layer, pair, w_qkv, qv_bias):
    outs = [shape((2, pair[0].shape[0], w_qkv.shape[2]), BF)] * 3
    return kernel_call(
        functools.partial(project_kernel, layer), "project", outs, 1_000_000_000, *pair, w_qkv, qv_bias
    )


def rows_of_page(refs, page, size):
    at = pl.ds(pl.multiple_of(page * size, size), size)
    return jnp.concatenate([ref[i, at, :] for ref in refs for i in range(2)], axis=0)


def attend(layer, start, q_ref, k_refs, v_refs, rel_ref, pad_ref, wo_ref, out_refs, pb_ref, o_ref):
    pages, heads, count = pb_ref.shape[:3]
    size = count // 2

    def step(page, carry):
        masks = head_masks(heads, BF)
        q = rows_of_page((q_ref,), page, size)
        k, v = rows_of_page(k_refs, page, size), rows_of_page(v_refs, page, size)
        o = jnp.zeros(q.shape, F32)
        for h in range(heads):
            rel = rel_ref[layer, h, start : start + count, :].astype(F32)
            s = mxu(q * masks[h], k, NT) + (rel + pad_ref[page])
            e = jnp.exp(s - jnp.max(s, axis=-1, keepdims=True))
            pb = (e * (1.0 / jnp.sum(e, axis=-1, keepdims=True))).astype(BF)
            pb_ref[page, h] = pb
            o = o + mxu(pb, v * masks[h], NN)
        o = o.astype(BF)
        o_ref[page] = o
        mixed = mxu(o, wo_ref[layer], NN).astype(BF)
        at = pl.ds(pl.multiple_of(page * size, size), size)
        out_refs[0][at, :], out_refs[1][at, :] = mixed[:size], mixed[size:]
        return carry

    lax.fori_loop(0, pages, step, 0, unroll=2)


def attention_far_kernel(
    layer, x2, x3, kn, vn, w_ref, bias_ref, rel_ref, pad_ref, wo_ref, p2, p3, qf, kf, vf, pb_ref, o_ref
):
    project_pair(layer, x2, x3, w_ref, bias_ref, (qf, kf, vf))
    start = rel_ref.shape[2] // 2
    attend(layer, start, qf, (kn, kf), (vn, vf), rel_ref, pad_ref, wo_ref, (p2, p3), pb_ref, o_ref)


def attention_near_kernel(layer, qn, kn, vn, kf, vf, rel_ref, pad_ref, wo_ref, p0, p1, pb_ref, o_ref):
    attend(layer, 0, qn, (kn, kf), (vn, vf), rel_ref, pad_ref, wo_ref, (p0, p1), pb_ref, o_ref)


def attention_outs(block, pad_bias, rel_bias):
    pages, unused, length = pad_bias.shape
    heads = rel_bias.shape[1]
    outs = [shape((pages, heads, length // 2, length), BF), shape((pages, length // 2, heads * HEAD_DIM), BF)]
    return [shape(block, BF)] * 2, outs


def attention_far(layer, pair, near, w_qkv, qv_bias, rel_bias, pad_bias, w_out):
    sums, saved = attention_outs(pair[0].shape, pad_bias, rel_bias)
    made = kernel_call(
        functools.partial(attention_far_kernel, layer),
        "attention_far",
        sums + [shape(near[0].shape, BF)] * 3 + saved,
        4_000_000_000,
        *pair,
        *near[1:],
        w_qkv,
        qv_bias,
        rel_bias,
        pad_bias,
        w_out,
    )
    return made[:2], made[2:5], made[5:]


def attention_near(layer, block, near, far, rel_bias, pad_bias, w_out):
    sums, saved = attention_outs(block, pad_bias, rel_bias)
    made = kernel_call(
        functools.partial(attention_near_kernel, layer),
        "attention_near",
        sums + saved,
        3_000_000_000,
        *near,
        *far[1:],
        rel_bias,
        pad_bias,
        w_out,
    )
    return made[:2], made[2:]


def attention_back_kernel(
    layer, g0, g1, g2, g3, qn, kn, vn, qf, kf, vf, pbn, pbf, w_ref, wo_ref, p0, p1, p2, p3, stack_ref, total_ref, sums_ref
):
    pages, heads = pbn.shape[:2]
    size = g0.shape[0] // pages
    total_ref[...] = jnp.zeros(total_ref.shape, F32)
    sums_ref[...] = jnp.zeros(sums_ref.shape, F32)

    def step(page, carry):
        masks = head_masks(heads, BF)
        rows = page_rows((g0, g1, g2, g3), page, size)
        go = mxu(rows, wo_ref[layer], NT).astype(BF)
        q, k, v = [rows_of_page(refs, page, size) for refs in ((qn, qf), (kn, kf), (vn, vf))]
        gq = gk = gv = jnp.zeros(q.shape, F32)
        for h in range(heads):
            pb = jnp.concatenate([pbn[page, h], pbf[page, h]], axis=0)
            go_h = go * masks[h]
            gv = gv + mxu(pb, go_h, TN)
            gp = mxu(go_h, v, NT)
            p = pb.astype(F32)
            gs = (p * (gp - jnp.sum(p * gp, axis=-1, keepdims=True))).astype(BF)
            total_ref[h] += gs.astype(F32)
            gq = gq + mxu(gs, k * masks[h], NN)
            gk = gk + mxu(gs, q * masks[h], TN)
        gq = (gq.astype(BF).astype(F32) * HEAD_DIM**-0.5).astype(BF)
        gk, gv = gk.astype(BF), gv.astype(BF)
        stack_ref[page, 0], stack_ref[page, 1], stack_ref[page, 2] = gq, gk, gv
        sums_ref[0] += fold_rows(gq.astype(F32))
        sums_ref[1] += fold_rows(gv.astype(F32))
        ga = mxu(gq, w_ref[layer, 0], NN) + mxu(gk, w_ref[layer, 1], NN) + mxu(gv, w_ref[layer, 2], NN)
        put_page((p0, p1, p2, p3), page, size, ga.astype(BF))
        return carry

    lax.fori_loop(0, pages, step, 0, unroll=2)


def attention_back(layer, blocks, kept, w_qkv, w_out):
    near, far, (pbn, unused), (pbf, unused) = kept
    pages, heads, unused, length = pbn.shape
    local = heads * HEAD_DIM
    outs = [shape(blocks[0].shape, BF)] * 4
    outs += [shape((pages, 3, length, local), BF), shape((heads, length, length), F32), shape((2, 8, local), F32)]
    made = kernel_call(
        functools.partial(attention_back_kernel, layer),
        "attention_back",
        outs,
        9_000_000_000,
        *blocks,
        *near,
        *far,
        pbn,
        pbf,
        w_qkv,
        w_out,
    )
    return made[:4], made[4:]


def attention_grads_kernel(*refs):
    rows_refs, grad_refs, refs = refs[:4], refs[4:8], refs[8:]
    stack_ref, on_ref, of_ref, place_ref, keep_ref, send_ref, acc_ref = refs
    pages, parts, length, local = stack_ref.shape
    size = rows_refs[0].shape[0] // pages
    acc_ref[...] = jnp.zeros(acc_ref.shape, F32)

    def step(page, carry):
        rows = page_rows(rows_refs, page, size)
        grad = page_rows(grad_refs, page, size)
        acc_ref[:local] += mxu(jnp.concatenate([on_ref[page], of_ref[page]], axis=0), grad, TN)
        for t in range(parts):
            acc_ref[(t + 1) * local : (t + 2) * local] += mxu(stack_ref[page, t], rows, TN)
        return carry

    lax.fori_loop(0, pages, step, 0, unroll=2)
    half = keep_ref.shape[0]
    mine = place_ref[0] & 1
    keep_ref[...] = acc_ref[pl.ds(pl.multiple_of(mine * half, half), half), :].astype(BF)
    send_ref[...] = acc_ref[pl.ds(pl.multiple_of((1 - mine) * half, half), half), :].astype(BF)


def attention_grads(rows, grads, stack, o, place):
    local, width = o[0].shape[-1], rows[0].shape[-1]
    return kernel_call(
        attention_grads_kernel,
        "attention_grads",
        [shape((2 * local, width), BF)] * 2,
        3_000_000_000,
        *rows,
        *grads,
        stack,
        *o,
        scalar(place),
        scratch=[pltpu.VMEM((4 * local, width), F32)],
    )


def gelu_parts(u):
    square = u * u
    t = jnp.tanh(GELU_SCALE * (u + GELU_CUBE * (square * u)))
    plus = 0.5 * (1.0 + t)
    slope = plus + 0.5 * u * (1.0 - t * t) * (GELU_SCALE * (1.0 + (3.0 * GELU_CUBE) * square))
    return u * plus, slope


def up_rows(layer, rows, up_ref, bias_ref):
    u = mxu(rows, up_ref[layer], NN) + of_layer(bias_ref, layer)
    z, slope = gelu_parts(u)
    return z.astype(BF), slope


def forward_kernel(layer, c0, c1, up_ref, bias_ref, down_ref, p0, p1, z_ref, slope_ref):
    for block, (rows_ref, out_ref) in enumerate(((c0, p0), (c1, p1))):
        z, slope = up_rows(layer, rows_ref[...], up_ref, bias_ref)
        z_ref[block], slope_ref[block] = z, slope.astype(BF)
        out_ref[...] = mxu(z, down_ref[layer], NN).astype(BF)


def feed_forward(layer, pair, w_up, up_bias, w_down):
    units = w_up.shape[2]
    size = pair[0].shape[0]
    outs = [shape(pair[0].shape, BF)] * 2 + [shape((2, size, units), BF)] * 2
    made = kernel_call(
        functools.partial(forward_kernel, layer), "feed_forward", outs, 2_000_000_000, *pair, w_up, up_bias, w_down
    )
    return made[:2], made[2], made[3]


def down_kernel(layer, zn_ref, zf_ref, down_ref, *out_refs):
    for block, out_ref in enumerate(out_refs):
        out_ref[...] = mxu((zn_ref, zf_ref)[block // 2][block % 2], down_ref[layer], NN).astype(BF)


def down_product(layer, z, w_down):
    outs = [shape((z[0].shape[1], w_down.shape[2]), BF)] * 4
    return kernel_call(functools.partial(down_kernel, layer), "down_product", outs, 1_500_000_000, *z, w_down)


def back_kernel(layer, g0, g1, g2, g3, sn_ref, sf_ref, up_ref, down_ref, p0, p1, p2, p3, gu_ref, sums_ref):
    sums_ref[...] = jnp.zeros(sums_ref.shape, F32)
    for block, (grad_ref, out_ref) in enumerate(zip((g0, g1, g2, g3), (p0, p1, p2, p3))):
        gz = mxu(grad_ref[...], down_ref[layer], NT)
        gu = (gz * (sn_ref, sf_ref)[block // 2][block % 2].astype(F32)).astype(BF)
        gu_ref[block] = gu
        sums_ref[...] += fold_rows(gu.astype(F32))
        out_ref[...] = mxu(gu, up_ref[layer], NT).astype(BF)


def feed_back(layer, blocks, slope, w_up, w_down):
    size, units = blocks[0].shape[0], w_up.shape[2]
    outs = [shape(blocks[0].shape, BF)] * 4 + [shape((4, size, units), BF), shape((8, units), F32)]
    made = kernel_call(
        functools.partial(back_kernel, layer), "feed_back", outs, 4_000_000_000, *blocks, *slope, w_up, w_down
    )
    return made[:4], made[4:]


def feed_grads_into(rows_refs, grad_refs, z_of, gu_of, place_ref, out_refs, both_ref):
    unused, units, width = both_ref.shape
    step = 256
    for start in range(0, units, step):
        rows = slice(start, start + step)
        down = sum(mxu(z_of(i, rows), g[...], TN) for i, g in enumerate(grad_refs))
        both_ref[0, rows, :] = down.astype(BF)
        up = sum(mxu(c[:, rows], gu_of(i), TN) for i, c in enumerate(rows_refs))
        both_ref[1, rows, :] = up.astype(BF)
    mine = place_ref[0] & 1
    parts = len(out_refs) // 2
    size = units // parts
    for part in range(parts):
        rows = slice(part * size, (part + 1) * size)
        out_refs[2 * part][...] = both_ref[mine, rows, :]
        out_refs[2 * part + 1][...] = both_ref[1 - mine, rows, :]


def feed_grads_kernel(*refs):
    zn, zf, gu, place_ref = refs[8:12]

    def z_of(i, rows):
        return (zn, zf)[i // 2][i % 2, :, rows]

    feed_grads_into(refs[:4], refs[4:8], z_of, lambda i: gu[i], place_ref, refs[12:-1], refs[-1])


def feed_grads(rows, grads, z, gu, place, parts):
    units, width = gu.shape[-1], rows[0].shape[-1]
    made = kernel_call(
        feed_grads_kernel,
        "feed_grads",
        [shape((units // parts, width), BF)] * (2 * parts),
        4_000_000_000,
        *rows,
        *grads,
        *z,
        gu,
        scalar(place),
        scratch=[pltpu.VMEM((2, units, width), BF)],
    )
    return [made[2 * i : 2 * i + 2] for i in range(parts)]


def both_pair(layer, rows_refs, grad_refs, up_ref, bias_ref, down_ref, out_refs, z_ref, gu_ref, sums_ref):
    for block in range(2):
        gz = mxu(grad_refs[block][...], down_ref[layer], NT)
        z, slope = up_rows(layer, rows_refs[block][...], up_ref, bias_ref)
        z_ref[block] = z
        gu = (gz * slope).astype(BF)
        gu_ref[block] = gu
        sums_ref[...] += fold_rows(gu.astype(F32))
        out_refs[block][...] = mxu(gu, up_ref[layer], NT).astype(BF)


def both_near_kernel(layer, c0, c1, g0, g1, up_ref, bias_ref, down_ref, p0, p1, z_ref, gu_ref, sums_ref):
    sums_ref[...] = jnp.zeros(sums_ref.shape, F32)
    weights = (up_ref, bias_ref, down_ref)
    both_pair(layer, (c0, c1), (g0, g1), *weights, (p0, p1), z_ref, gu_ref, sums_ref)


def both_far_kernel(layer, *refs):
    rows_refs, grad_refs, refs = refs[:4], refs[4:8], refs[8:]
    zn, gun, sums_near, up_ref, bias_ref, down_ref, place_ref, p2, p3, z_ref, sums_ref, keep_ref, send_ref = refs[:13]
    gu_ref, both_ref = refs[13:]
    sums_ref[...] = sums_near[...]
    weights = (up_ref, bias_ref, down_ref)
    both_pair(layer, rows_refs[2:], grad_refs[2:], *weights, (p2, p3), z_ref, gu_ref, sums_ref)

    def z_of(i, rows):
        return (zn, z_ref)[i // 2][i % 2, :, rows]

    def gu_of(i):
        return (gun, gu_ref)[i // 2][i % 2]

    feed_grads_into(rows_refs, grad_refs, z_of, gu_of, place_ref, (keep_ref, send_ref), both_ref)


def both_near(layer, rows, grads, w_up, up_bias, w_down):
    size, units = rows[0].shape[0], w_up.shape[2]
    outs = [shape(rows[0].shape, BF)] * 2 + [shape((2, size, units), BF)] * 2 + [shape((8, units), F32)]
    made = kernel_call(
        functools.partial(both_near_kernel, layer),
        "both_near",
        outs,
        3_000_000_000,
        *rows,
        *grads,
        w_up,
        up_bias,
        w_down,
    )
    return made[:2], made[2:]


def both_far(layer, rows, grads, near, w_up, up_bias, w_down, place):
    size, units = rows[0].shape[0], w_up.shape[2]
    width = rows[0].shape[1]
    outs = [shape(rows[0].shape, BF)] * 2 + [shape((2, size, units), BF), shape((8, units), F32)]
    outs += [shape((units, width), BF)] * 2
    made = kernel_call(
        functools.partial(both_far_kernel, layer),
        "both_far",
        outs,
        7_000_000_000,
        *rows,
        *grads,
        *near,
        w_up,
        up_bias,
        w_down,
        scalar(place),
        scratch=[pltpu.VMEM((2, size, units), BF), pltpu.VMEM((2, units, width), BF)],
    )
    return made[:2], made[2], made[3], made[4:]


def partners(bits, bit):
    return [(i, i ^ (1 << bit)) for i in range(1 << len(bits))]


def crossed(place, swapped):
    other = (place & ~3) | ((place & 1) << 1) | ((place >> 1) & 1)
    return jnp.where(swapped == 1, other, place)


def crossed_partners(bits, bit, crossing):
    pairs = []
    for i in range(1 << len(bits)):
        for t in range(4):
            taken = bit ^ 1 if crossing and bit < 2 and t & 1 else bit
            pairs.append((i * 4 + t, (i ^ (1 << taken)) * 4 + t))
    return pairs


def halve_kernel(bit, keep_ref, got_ref, place_ref, out_keep_ref, out_send_ref):
    half = out_keep_ref.shape[0]
    mine = (place_ref[0] >> bit) & 1
    for out_ref, which in ((out_send_ref, 1 - mine), (out_keep_ref, mine)):
        at = pl.ds(pl.multiple_of(which * half, half), half)
        out_ref[...] = (keep_ref[at, :].astype(F32) + got_ref[at, :].astype(F32)).astype(BF)


def halve(keep, got, bit, place):
    rows, width = keep.shape
    outs = [shape((rows // 2, width), BF)] * 2
    return kernel_call(
        functools.partial(halve_kernel, bit), "halve", outs, 200_000_000, keep, got, scalar(place)
    )


def join_kernel(bit, own_ref, got_ref, place_ref, out_ref):
    half = own_ref.shape[0]
    mine = (place_ref[0] >> bit) & 1
    out_ref[pl.ds(pl.multiple_of(mine * half, half), half), :] = own_ref[...]
    out_ref[pl.ds(pl.multiple_of((1 - mine) * half, half), half), :] = got_ref[...]


def join(own, got, bit, place):
    rows, width = own.shape
    return kernel_call(
        functools.partial(join_kernel, bit),
        "join",
        [shape((2 * rows, width), BF)],
        200_000_000,
        own,
        got,
        scalar(place),
    )[0]


class PageSum:
    def __init__(self, halves, bits, places, crossing):
        self.own, send = halves
        self.bits, self.place, self.crossing = bits, places[crossing], crossing
        self.plan = [self.cut, self.add, self.turn, self.back]
        self.got = self.swap(send, 0)

    def swap(self, values, bit):
        self.sent = values
        return lax.ppermute(values, ("dp", "tensor"), crossed_partners(self.bits, bit, self.crossing))

    def cut(self, got):
        self.own, send = halve(self.own, got, 1, self.place)
        return self.swap(send, 1)

    def add(self, got):
        self.own = self.own + got
        return self.swap(self.own, 2)

    def turn(self, got):
        self.own = self.own + got
        for bit in self.bits[3:]:
            self.own = self.own + self.swap(self.own, bit)
        return self.swap(self.own, 1)

    def back(self, got):
        self.own = join(self.own, got, 1, self.place)
        return self.swap(self.own, 0)

    def step(self, token):
        self.got = self.plan.pop(0)(tied(self.got, token))
        return self.sent

    def ended(self):
        return self.own, self.got


def sum_small(values, axis, bits, count):
    for bit in bits:
        values = values + lax.ppermute(values, axis, partners(range(count), bit))
    return values


def row_sum(values):
    return jnp.sum(values, axis=0, keepdims=True)


def pack_rows_kernel(ones0, twos0, ones1, twos1, last_ref, out_ref):
    out_ref[...] = jnp.zeros(out_ref.shape, F32)
    for layer, (one_ref, two_ref) in enumerate(((ones0, twos0), (ones1, twos1))):
        down = ones1[2] if layer == 0 else last_ref[...]
        members = [one_ref[0], one_ref[1], two_ref[2], two_ref[0], two_ref[1], down]
        for i, member in enumerate(members):
            out_ref[2 * i + layer : 2 * i + layer + 1, :] = row_sum(member)
    out_ref[12:13, :] = row_sum(ones0[2])


def pack_rows(ones, twos, last):
    return kernel_call(
        pack_rows_kernel,
        "pack_rows",
        [shape((16, last.shape[-1]), F32)],
        1_000_000,
        ones[0],
        twos[0],
        ones[1],
        twos[1],
        last,
    )[0]


def pack_all_kernel(rows_ref, qv0, qv1, up0, up1, rel0, rel1, out_ref):
    local = qv0.shape[-1]
    out_ref[:16, :] = rows_ref[...]
    out_ref[16:, :] = jnp.zeros((32, out_ref.shape[1]), F32)
    for layer, (qv_ref, up_ref, rel_ref) in enumerate(((qv0, up0, rel0), (qv1, up1, rel1))):
        out_ref[16 + layer : 17 + layer, :] = row_sum(up_ref[...])
        for i in range(2):
            out_ref[18 + 2 * layer + i : 19 + 2 * layer + i, :local] = row_sum(qv_ref[i])
        heads = rel_ref.shape[0] // 24
        for h in range(heads):
            start = (layer * heads + h) * 128
            out_ref[24:48, start : start + 32] = rel_ref[h * 24 : h * 24 + 24, :]


def pack_all(rows, qv_sums, up_sums, rel_sums):
    return kernel_call(
        pack_all_kernel,
        "pack_all",
        [shape((48, rows.shape[-1]), F32)],
        1_000_000,
        rows,
        *qv_sums,
        *up_sums,
        *rel_sums,
    )[0]


def unpack_kernel(all_ref, *out_refs):
    rows, mask_ref, up_ref, qv_ref, rel_ref = out_refs[:6], *out_refs[6:]
    for i, row_ref in enumerate(rows):
        row_ref[...] = all_ref[2 * i : 2 * i + 2, :]
    mask_ref[...] = all_ref[12:13, :]
    up_ref[...] = all_ref[16:18, :]
    heads, layers, entries = rel_ref.shape
    local = qv_ref.shape[-1]
    for layer in range(layers):
        qv_ref[layer] = all_ref[18 + 2 * layer : 20 + 2 * layer, :local]
        for h in range(heads):
            start = (layer * heads + h) * 128
            for j in range(6):
                lines = [all_ref[24 + 4 * j + r : 25 + 4 * j + r, start : start + 32] for r in range(4)]
                size = min(128, entries - 128 * j)
                line = jnp.concatenate(lines, axis=1)[:, :size]
                rel_ref[h, layer : layer + 1, 128 * j : 128 * j + size] = line


def unpack(values, heads, entries):
    width = values.shape[-1]
    outs = [shape((LAYERS, width), F32)] * 6 + [shape((1, width), F32), shape((LAYERS, width), F32)]
    outs += [shape((LAYERS, 2, heads * HEAD_DIM), F32), shape((heads, LAYERS, entries), F32)]
    return kernel_call(unpack_kernel, "unpack", outs, 1_000_000, values)


def assemble_kernel(layer, pieces, own_ref, got_ref, place_ref, *refs):
    out_refs, (stage_ref, sems) = refs[-2 - len(pieces) : -2], refs[-2:]
    half = own_ref.shape[0]
    mine = place_ref[0] & 1
    stage_ref[pl.ds(pl.multiple_of(mine * half, half), half), :] = own_ref[...].astype(F32)
    stage_ref[pl.ds(pl.multiple_of((1 - mine) * half, half), half), :] = got_ref[...].astype(F32)
    copies = []
    for out_ref, parts in zip(out_refs, pieces):
        for index, start, rows in parts:
            target = out_ref.at[(layer,) + index]
            source = stage_ref.at[pl.ds(start, rows), :]
            copies.append(pltpu.make_async_copy(source, target, sems.at[len(copies)]))
    for copy in copies:
        copy.start()
    for copy in copies:
        copy.wait()


def assemble(layer, name, pieces, outs, own, got, place, before):
    rows, width = own.shape
    anywhere = pl.BlockSpec(memory_space=pl.ANY)
    count = sum(len(parts) for parts in pieces)
    return pl.pallas_call(
        functools.partial(assemble_kernel, layer, pieces),
        out_shape=tuple(outs),
        in_specs=[VMEM, VMEM, pl.BlockSpec(memory_space=pltpu.SMEM)] + [anywhere] * len(before),
        out_specs=tuple([anywhere] * len(outs)),
        scratch_shapes=[pltpu.VMEM((2 * rows, width), F32), pltpu.SemaphoreType.DMA((count,))],
        input_output_aliases={3 + i: i for i in range(len(before))},
        name=name,
        compiler_params=pltpu.CompilerParams(vmem_limit_bytes=VMEM_GRANT),
        cost_estimate=pl.CostEstimate(flops=1_000_000, bytes_accessed=rows * width, transcendentals=0),
    )(own, got, place, *before)


def assemble_feed(layer, part, parts, sums, place, before=()):
    own, got = sums.ended()
    size, width = own.shape
    pieces = [[((pl.ds(part * size, size),), 0, size)], [((pl.ds(part * size, size),), size, size)]]
    outs = [shape((LAYERS, parts * size, width), F32)] * 2
    return assemble(layer, "assemble_feed", pieces, outs, own, got, place, before)


def assemble_attention(layer, sums, place, before=()):
    own, got = sums.ended()
    local, width = own.shape[0] // 2, own.shape[1]
    pieces = [[((), 0, local)], [((t,), (t + 1) * local, local) for t in range(3)]]
    outs = [shape((LAYERS, local, width), F32), shape((LAYERS, 3, local, width), F32)]
    return assemble(layer, "assemble_attention", pieces, outs, own, got, place, before)


def shards(
    n_dp,
    patch_rows,
    cotangent,
    mask_flags,
    pad_flags,
    buckets,
    mask_emb,
    ln1_gain,
    ln1_bias,
    w_qkv,
    qv_bias,
    rel_table,
    w_out,
    out_bias,
    ln2_gain,
    ln2_bias,
    w_up,
    up_bias,
    w_down,
    down_bias,
):
    member = lax.axis_index("tensor").reshape(1).astype(jnp.int32)
    straight = lax.axis_index("dp").reshape(1).astype(jnp.int32)
    places = [straight, crossed(straight, lax.axis_index("tensor") & 1)]
    bits = list(range(n_dp.bit_length() - 1))
    pages = patch_rows.shape[1]
    heads, entries = rel_table.shape[1:]
    last = LAYERS - 1
    masked = mask_flags.T
    w_qkv = jnp.swapaxes(w_qkv, 2, 3)

    hidden, own, last_own, last_sum = first_norm(
        patch_rows, cotangent, masked, mask_emb.reshape(1, -1), ln1_gain, ln1_bias
    )
    rel_bias, ordered, pad_bias = bias_of_buckets(jnp.swapaxes(rel_table, 0, 1), buckets, pad_flags.T, member)
    last_blocks = None
    kept = []
    for layer in range(LAYERS):
        before = hidden
        near, far = swap_core(own), swap_chip(own)
        q_near = project(layer, (own, near), w_qkv, qv_bias)
        far = tied(far, (q_near, rel_bias))
        rows_one = [own, near, far, swap_core(far)]
        if last_blocks is None:
            last_blocks = spread(tied(last_own, rows_one[3]))
        other, q_far, saved_far = attention_far(
            layer, rows_one[2:], q_near, w_qkv, qv_bias, rel_bias, pad_bias, w_out
        )
        sent = other[0] + swap_core(other[1])
        arriving = swap_chip(sent)
        mine, saved_near = attention_near(
            layer, own.shape, [tied(q_near[0], sent), *q_near[1:]], q_far, rel_bias, pad_bias, w_out
        )
        terms = [mine[0], swap_core(mine[1]), tied(arriving, mine)]
        middle, own = add_norm(hidden, terms, (layer, layer), out_bias, ln2_gain, ln2_bias)
        saved = (q_near, q_far, saved_near, saved_far)
        near, far = swap_core(own), swap_chip(own)
        if layer == last:
            partial, near_made = both_near(layer, (own, near), last_blocks[:2], w_up, up_bias, w_down)
            far = tied(far, near_made)
            rows_two = [own, near, far, swap_core(far)]
            other, z, up_sums, mlp = both_far(
                layer, rows_two, last_blocks, near_made, w_up, up_bias, w_down, places[1]
            )
            partial = [*partial, *other]
            kept.append((rows_one, before, saved, middle, rows_two, (near_made[0], z), None))
        else:
            partial, *near_made = feed_forward(layer, (own, near), w_up, up_bias, w_down)
            far = tied(far, near_made)
            rows_two = [own, near, far, swap_core(far)]
            other, *far_made = feed_forward(layer, rows_two[2:], w_up, up_bias, w_down)
            z, slope = zip(near_made, far_made)
            kept.append((rows_one, before, saved, middle, rows_two, z, slope))
            near, far, unused = collect([*partial, *other])
            hidden, own = add_norm(middle, near + [far], (layer, layer + 1), down_bias, ln1_gain, ln1_bias)

    rows_one, before, saved, middle, rows_two, z, unused = kept[last]
    near, far, sent = collect(partial)
    mlp1 = PageSum(mlp, bits, places, 1)
    g1, low, twos1 = norm_back(last_own, near + [far], middle, last, ln2_gain)
    result_parts = down_product(last, (tied(z[0], low), z[1]), w_down)
    token = mlp1.step(result_parts[0])
    out_blocks = spread(low, (result_parts, token))
    partial, (stack, totals, qv1) = attention_back(last, out_blocks, saved, w_qkv, w_out)
    near, far, sent = collect(partial)
    mix = attention_grads(rows_one, out_blocks, tied(stack, sent), (saved[2][1], saved[3][1]), places[0])
    mix1 = PageSum(mix, bits, places, 0)
    token = mlp1.step(mix)
    far = tied(far, (token,))
    grad, low, ones1 = norm_back(g1, near + [far], before, last, ln1_gain)
    rel1 = sum_by_bucket(tied(totals, low), ordered)
    token = mix1.step(rel1)
    grad_blocks = spread(low, (token,))
    up1 = up_sums

    rows_one, before, saved, middle, rows_two, z, slope = kept[0]
    partial, (gu, up0) = feed_back(0, grad_blocks, slope, w_up, w_down)
    near, far, sent = collect(partial)
    mlp = feed_grads(rows_two, grad_blocks, z, tied(gu, sent), places[1], 2)
    mlp0a, mlp0b = [PageSum(x, bits, places, 1) for x in mlp]
    token = mix1.step(mlp)
    far = tied(far, (token,))
    g1, low, twos0 = norm_back(grad, near + [far], middle, 0, ln2_gain)
    token = mlp1.step(low)
    token = mlp0a.step(token)
    out_blocks = spread(low, (token,))
    partial, (stack, totals, qv0) = attention_back(0, out_blocks, saved, w_qkv, w_out)
    near, far, sent = collect(partial)
    mix = attention_grads(rows_one, out_blocks, tied(stack, sent), (saved[2][1], saved[3][1]), places[1])
    mix0 = PageSum(mix, bits, places, 1)
    token = mlp1.step(mix)
    token = mlp0b.step(token)
    token = mix1.step(token)
    far = tied(far, (token,))
    grad, ones0 = last_norm_back(g1, near + [far], before, ln1_gain, masked)

    def hop(values, axis, order, bit):
        return lax.ppermute(values, axis, partners(order, bit))

    rows = pack_rows((ones0, ones1), (twos0, twos1), last_sum)
    rows_got = hop(rows, "tensor", [0, 1], 0)
    token = rows
    token = mlp0a.step(token)
    token = mlp0b.step(token)
    token = mix0.step(token)
    rows = token = rows + tied(rows_got, token)
    rows_got = hop(rows, "tensor", [0, 1], 1)
    rel0 = token = sum_by_bucket(tied(totals, token), ordered)
    result_near, result_far, unused = collect([tied(p, rel0) for p in result_parts])
    small = pack_all(rows + tied(rows_got, token), (qv0, qv1), (up0, up1), (rel0, rel1))
    small_got = hop(small, "dp", bits, 0)
    token = small
    token = mlp0a.step(token)
    token = mlp0b.step(token)
    token = mix0.step(token)
    small = token = small + tied(small_got, token)
    small_got = hop(small, "dp", bits, 1)
    token = mix1.step(token)
    result = token = last_result(
        kept[last][3], result_near + [tied(result_far, token)], last, down_bias, pages
    )
    token = mlp0a.step(token)
    small = token = small + tied(small_got, token)
    small_got = hop(small, "dp", bits, 2)
    token = mlp0b.step(token)
    d_mlp = assemble_feed(last, 0, 1, mlp1, tied(places[1], token))
    token = d_mlp[0]
    token = mix0.step(token)
    small = small + tied(small_got, token)
    small = token = sum_small(small, "dp", bits[3:], len(bits))
    d_mlp = assemble_feed(0, 0, 2, mlp0a, tied(places[1], token), d_mlp)
    token = d_mlp[0]
    d_mix = assemble_attention(last, mix1, tied(places[0], token))
    token = d_mix[0]
    token = mix0.step(token)
    d_mlp = assemble_feed(0, 1, 2, mlp0b, tied(places[1], token), d_mlp)
    token = d_mlp[0]
    d_mix = assemble_attention(0, mix0, tied(places[1], token), d_mix)
    token = d_mix[0]
    small = unpack(small, heads, entries)
    d_ln1_gain, d_ln1_bias, d_out_bias, d_ln2_gain, d_ln2_bias, d_down_bias, d_mask, d_up_bias, d_qv, d_rel = small
    return (
        result,
        grad,
        d_mask.reshape(-1),
        d_ln1_gain,
        d_ln1_bias,
        jnp.swapaxes(d_mix[1], 2, 3),
        d_qv,
        jnp.swapaxes(d_rel, 0, 1),
        d_mix[0],
        d_out_bias,
        d_ln2_gain,
        d_ln2_bias,
        d_mlp[1],
        d_up_bias,
        d_mlp[0],
        d_down_bias,
    )


def solution(mesh):
    rows = P("tensor", "dp", None)
    units = P(None, "tensor", None)
    columns = P(None, None, "tensor")
    whole = P()
    return jax.shard_map(
        functools.partial(shards, mesh.shape["dp"]),
        mesh=mesh,
        in_specs=(
            rows,
            rows,
            P("tensor", "dp"),
            P(None, "dp"),
            whole,
            whole,
            whole,
            whole,
            P(None, None, None, "tensor"),
            columns,
            units,
            units,
            whole,
            whole,
            whole,
            columns,
            P(None, "tensor"),
            units,
            whole,
        ),
        out_specs=(
            rows,
            rows,
            whole,
            whole,
            whole,
            P(None, None, None, "tensor"),
            columns,
            units,
            units,
            whole,
            whole,
            whole,
            columns,
            P(None, "tensor"),
            units,
            whole,
        ),
        check_vma=False,
    )
```
